32 devices in a mesh: scene: 2 (over x), row: 16 (over z, y, core).
Axes of the slice: x: 2, y: 2, z: 4, core: 2. Of those that a mesh axis runs over, the one named last changes fastest.
Arguments:
- echoes: bfloat16 [2048, 2, 8192], P(('scene', 'row')), parts along dimension 0, may hold values from -6 to 6
- range_replica: bfloat16 [2, 1024], replicated, may hold values from -0.125 to 0.125
- azimuth_replicas: bfloat16 [16, 2, 512], replicated, may hold values from -0.1875 to 0.1875
- replica_index: int32 [16384], P(('scene', 'row')), parts along dimension 0, may hold values from 0 to 15
- azimuth_extent: int32 [128], P('scene'), parts along dimension 0, may hold values from 0 to 16
- range_extent: int32 [1024], P('scene'), parts along dimension 0, may hold values from 0 to 16
Outputs:
- focused: bfloat16 [2048, 2, 8192], P('scene', None, 'row'), parts along dimension 0
- looked: float32 [1024, 64], P(('scene', 'row')), parts along dimension 0
The draws below stay inside these ranges and needn't reach their ends.
There are 2 independent parts, one for each index of `scene`. The reference program is written for one: setup_inputs(seed, part) draws one part's arguments, and reference() takes and returns one part's arrays. A program takes and returns all parts, laid end to end along the dimension named above; an argument that names none is the same for every part. Nothing has to cross between parts.
All inputs are finite; a program needn't handle non-finite values.
Results may differ from the reference program's by a relative error of at most 0.0049.
Values may be sent and summed in bfloat16 or wider, within the bound.
No kernel may reach another device: no remote copies, remote signals or barrier semaphores. Data moves between devices by JAX's collectives and lax.ppermute only.
A program may use at most 128 MiB of HBM per device.

```python
import jax
import jax.numpy as jnp
from jax import lax

P_SIZE = 1024
S = 8192
K_RG = 1024
K_AZ = 512
NF = 16
TILE = 16
EXT = 16


def extent_values(key, count, salt):
    base_key = jax.random.fold_in(key, salt)
    values = jax.random.randint(jax.random.fold_in(base_key, 1), (count,), 0, EXT + 1, dtype=jnp.int32)
    spots = jax.random.permutation(jax.random.fold_in(base_key, 2), count)
    return values.at[spots[0]].set(EXT).at[spots[1]].set(0)


def draw_azimuth_extent(key, part):
    return extent_values(key, P_SIZE // TILE, 7)


def draw_range_extent(key, part):
    return extent_values(key, S // TILE, 9)


def with_ends(values, stream_key, smallest, largest):
    longest = values.shape.index(max(values.shape))
    spots = []
    for shift in (0, 1):
        where = [jax.random.randint(jax.random.fold_in(stream_key, axis), (), 0, length) for axis, length in enumerate(values.shape)]
        where[longest] = (where[longest] + shift) % values.shape[longest]
        spots.append(tuple(where))
    return values.at[spots[0]].set(smallest).at[spots[1]].set(largest)


def block_levels(own_key, shape, shards, smallest, top_value):
    loudness = 1.0
    for position, blocks in shards:
        heights = jax.random.uniform(jax.random.fold_in(jax.random.fold_in(own_key, 6), position), (blocks,), jnp.float32, smallest / len(shards), top_value / len(shards))
        loudness = loudness * jnp.repeat(jnp.exp(heights), shape[position] // blocks).reshape((-1,) + (1,) * (len(shape) - 1 - position))
    return loudness


def gaussian(own_key, shape, spread, bound, shards=(), kind=jnp.bfloat16):
    drawn = spread * jax.random.normal(own_key, shape, jnp.float32)
    if shards:
        drawn = drawn * block_levels(own_key, shape, shards, -0.22, 0.18)
    return jnp.clip(drawn, -bound, bound).astype(kind)


def setup_inputs(seed: int = 0, part: int = 0) -> dict:
    arg_keys = jax.random.split(jax.random.key(seed), 7)
    part_keys = jax.random.split(jax.random.fold_in(arg_keys[6], part), 7)
    return {
        "echoes": gaussian(part_keys[0], (P_SIZE, 2, S), 1.0, 6.0, ((0, 16),)),
        "range_replica": gaussian(arg_keys[1], (2, K_RG), (2 * K_RG) ** -0.5, 0.125),
        "azimuth_replicas": gaussian(arg_keys[2], (NF, 2, K_AZ), (2 * K_AZ) ** -0.5, 0.1875),
        "replica_index": with_ends(jax.random.randint(part_keys[3], (S,), 0, NF), jax.random.fold_in(part_keys[3], 1), 0, NF - 1).astype(jnp.int32),
        "azimuth_extent": draw_azimuth_extent(jax.random.fold_in(jax.random.fold_in(arg_keys[6], part), 71), part),
        "range_extent": draw_range_extent(jax.random.fold_in(jax.random.fold_in(arg_keys[6], part), 71), part),
    }


HIGHEST = lax.Precision.HIGHEST


def window_mask(count_tiles, count_cells, extent):
    cells = jnp.arange(count_cells, dtype=jnp.int32)
    starts = jnp.arange(count_tiles, dtype=jnp.int32) * TILE - extent
    stops = starts + TILE + 2 * extent
    inside = (cells[None, :] >= starts[:, None]) & (cells[None, :] < stops[:, None])
    return inside.astype(jnp.float32)


def reference(echoes, range_replica, azimuth_replicas, replica_index, azimuth_extent, range_extent):
    pulses = echoes.shape[0]
    samples = echoes.shape[2]
    tap_count = range_replica.shape[1]
    padded_length = samples + tap_count
    signal = lax.complex(echoes[:, 0, :].astype(jnp.float32), echoes[:, 1, :].astype(jnp.float32))
    kernel = lax.complex(range_replica[0].astype(jnp.float32), range_replica[1].astype(jnp.float32))
    signal_spectrum = jnp.fft.fft(signal, n=padded_length, axis=1)
    kernel_spectrum = jnp.fft.fft(kernel, n=padded_length)
    compressed_full = jnp.fft.ifft(signal_spectrum * jnp.conj(kernel_spectrum)[None, :], axis=1)[:, :samples]
    comp_real = jnp.real(compressed_full).astype(jnp.bfloat16)
    comp_imag = jnp.imag(compressed_full).astype(jnp.bfloat16)
    comp_real, comp_imag = lax.optimization_barrier((comp_real, comp_imag))
    turned = lax.complex(comp_real.astype(jnp.float32), comp_imag.astype(jnp.float32))
    turned_spectrum = jnp.fft.fft(turned, axis=0)
    replicas = lax.complex(azimuth_replicas[:, 0, :].astype(jnp.float32), azimuth_replicas[:, 1, :].astype(jnp.float32))
    replica_spectra = jnp.fft.fft(replicas, n=pulses, axis=1)
    chosen = jnp.take(replica_spectra.T, replica_index, axis=1)
    azimuth = jnp.fft.ifft(turned_spectrum * jnp.conj(chosen), axis=0)
    az_real = jnp.real(azimuth)
    az_imag = jnp.imag(azimuth)
    focused = jnp.stack([az_real, az_imag], axis=1).astype(jnp.bfloat16)
    intensity = az_real * az_real + az_imag * az_imag
    pulse_mask = window_mask(pulses // TILE, pulses, azimuth_extent)
    range_mask = window_mask(samples // TILE, samples, range_extent)
    row_sums = jnp.dot(pulse_mask, intensity, precision=HIGHEST, preferred_element_type=jnp.float32)
    window_sums = jnp.dot(range_mask, row_sums.T, precision=HIGHEST, preferred_element_type=jnp.float32)
    counts = jnp.sum(range_mask, axis=1)[:, None] * jnp.sum(pulse_mask, axis=1)[None, :]
    looked = window_sums / counts
    return focused, looked
```

```python
import functools

import jax
import jax.numpy as jnp
import ml_dtypes
import numpy as np
from jax import lax
from jax.experimental import pallas as pl
from jax.experimental.pallas import tpu as pltpu
from jax.sharding import PartitionSpec as P

TILE = 16
RADIX = 4
F32 = jnp.float32
BF16 = jnp.bfloat16
VMEM_LIMIT = 56 << 20


def dot(a, b):
    return jnp.dot(a, b, preferred_element_type=F32)


def dot_nt(a, b):
    return lax.dot_general(a, b, (((1,), (1,)), ((), ())), preferred_element_type=F32)


def split(x):
    high = x.astype(BF16)
    low = (x - high.astype(F32)).astype(BF16)
    return high, low


@functools.lru_cache(maxsize=None)
def phase_matrices(length):
    part = length // RADIX
    k = np.arange(part)
    q = np.arange(RADIX)
    phase = (k[None, None, :] * (RADIX * k[None, :, None] + q[:, None, None])) % length
    angle = phase * (-2.0 * np.pi / length)
    re, im = np.cos(angle), np.sin(angle)
    full = np.concatenate([np.concatenate([re, -im], axis=2), np.concatenate([im, re], axis=2)], axis=1)

    def terms(matrix):
        high = matrix.astype(ml_dtypes.bfloat16)
        low = (matrix - high.astype(np.float64)).astype(ml_dtypes.bfloat16)
        return np.stack([high, low])

    return terms(full), terms(np.ascontiguousarray(full.transpose(0, 2, 1)))


def send_order(count):
    if count < 8:
        return list(range(1, count))
    quarter = count // 4
    order = []
    for low in range(quarter):
        order += [2 * quarter + low, 3 * quarter + low, quarter + low]
        if low:
            order.append(low)
    return order


def range_kernel(offsets, width, block, me_ref, x_ref, h_ref, *refs):
    outs, table = refs[:-1], refs[-1]
    rows = x_ref.shape[0]
    taps = h_ref.shape[1]
    count = x_ref.shape[2] // width
    replica = h_ref[...].astype(F32)
    for part in range(2):
        line = jnp.concatenate([replica[part : part + 1], jnp.zeros((1, block), F32)], axis=1)
        lines = jnp.broadcast_to(line, (block, taps + block))
        table[part] = pltpu.roll(lines, 0, 1, stride=1, stride_axis=0).astype(BF16)
    me = me_ref[0]
    for offset, out in zip(offsets, outs):
        owner = me ^ offset
        pieces = []
        for step in range(1 + -(-taps // width)):
            place = owner + step
            start = pl.multiple_of(jnp.minimum(place, count - 1) * width, width)
            piece = jnp.swapaxes(x_ref[:, :, pl.ds(start, width)], 0, 1)
            if step:
                piece = jnp.where(place < count, piece, jnp.zeros_like(piece))
            pieces.append(piece.reshape(2 * rows, width))
        window = jnp.concatenate(pieces, axis=1)
        subs = width // block
        stacked = jnp.concatenate(
            [window[:, j * block : j * block + block + taps] for j in range(subs)], axis=0
        )
        with_real = dot_nt(stacked, table[0])
        with_imag = dot_nt(stacked, table[1])
        for j in range(subs):
            at = 2 * rows * j
            re, im = slice(at, at + rows), slice(at + rows, at + 2 * rows)
            cells = slice(j * block, (j + 1) * block)
            out[0, :, cells] = (with_real[re] + with_imag[im]).astype(BF16)
            out[1, :, cells] = (with_real[im] - with_imag[re]).astype(BF16)


def compress(me, echoes, range_replica, offsets, width):
    rows = echoes.shape[0]
    taps = range_replica.shape[1]
    block = min(256, width)
    vmem = pl.BlockSpec(memory_space=pltpu.VMEM)
    flops = len(offsets) * 8 * rows * width * (taps + block)
    return pl.pallas_call(
        functools.partial(range_kernel, tuple(offsets), width, block),
        out_shape=[jax.ShapeDtypeStruct((2, rows, width), BF16)] * len(offsets),
        in_specs=[pl.BlockSpec(memory_space=pltpu.SMEM), vmem, vmem],
        out_specs=[vmem] * len(offsets),
        scratch_shapes=[pltpu.VMEM((2, block, taps + block), BF16)],
        compiler_params=pltpu.CompilerParams(vmem_limit_bytes=VMEM_LIMIT),
        cost_estimate=pl.CostEstimate(flops=flops, bytes_accessed=echoes.size * 4, transcendentals=0),
        name="range_compress",
    )(me, echoes, range_replica)


def butterfly(x, sign):
    (ar, ai), (br, bi), (cr, ci), (dr, di) = x
    pr, pi, mr, mi = ar + cr, ai + ci, ar - cr, ai - ci
    sr, si, tr, ti = br + dr, bi + di, br - dr, bi - di
    if sign < 0:
        tr, ti = ti, -tr
    else:
        tr, ti = -ti, tr
    return [(pr + sr, pi + si), (mr + tr, mi + ti), (pr - sr, pi - si), (mr - tr, mi - ti)]


def spectra_kernel(taps_ref, index_ref, matrix_ref, out_ref):
    part = matrix_ref.shape[-1] // 2
    length = part * RADIX
    replicas = taps_ref.shape[-1]
    width = index_ref.shape[1]
    tap_count = taps_ref.shape[1]
    zero = jnp.zeros((part, replicas), F32)
    pieces = []
    for q in range(RADIX):
        if (q + 1) * part <= tap_count:
            pieces.append(tuple(taps_ref[c, q * part : (q + 1) * part].astype(F32) for c in range(2)))
        else:
            pieces.append((zero, zero))
    chosen = lax.broadcasted_iota(jnp.int32, (replicas, width), 0) == index_ref[...]
    chosen = chosen.astype(F32).astype(BF16)
    for q, (re, im) in enumerate(butterfly(pieces, -1)):
        high, low = split(jnp.concatenate([re, im], axis=0))
        spectrum = dot(matrix_ref[0, q], high) + dot(matrix_ref[1, q], high) + dot(matrix_ref[0, q], low)
        high, low = split(spectrum * (1.0 / length))
        out_ref[q] = dot(high, chosen) + dot(low, chosen)


def azimuth_kernel(
    offsets, me_ref, forward_ref, inverse_ref, chosen_ref, pulse_ref, range_ref, *refs
):
    sources = refs[: len(offsets)]
    focused_ref, sums_ref, x_ref, v_ref, power_ref = refs[len(offsets) :]
    rows = sources[0].shape[1]
    length = x_ref.shape[1]
    part = length // RADIX
    me = me_ref[0]
    for offset, source in zip(offsets, sources):
        start = pl.multiple_of((me ^ offset) * rows, rows)
        for c in range(2):
            x_ref[c, pl.ds(start, rows), :] = source[c]
    x = [
        tuple(x_ref[c, q * part : (q + 1) * part, :].astype(F32) for c in range(2)) for q in range(RADIX)
    ]
    for q, (re, im) in enumerate(butterfly(x, -1)):
        high, low = split(jnp.concatenate([re, im], axis=0))
        spectrum = dot(forward_ref[0, q], high) + dot(forward_ref[1, q], high) + dot(forward_ref[0, q], low)
        sr, si = spectrum[:part], spectrum[part:]
        gr, gi = chosen_ref[q, :part], chosen_ref[q, part:]
        high, low = split(jnp.concatenate([sr * gr + si * gi, si * gr - sr * gi], axis=0))
        v_ref[q] = dot(inverse_ref[0, q], high) + dot(inverse_ref[1, q], high) + dot(inverse_ref[0, q], low)
    v = [(v_ref[q, :part], v_ref[q, part:]) for q in range(RADIX)]
    for q, (re, im) in enumerate(butterfly(v, 1)):
        span = slice(q * part, (q + 1) * part)
        both = jnp.stack([re.astype(BF16), im.astype(BF16)], axis=0)
        focused_ref[span] = jnp.swapaxes(both, 0, 1)
        high, low = split(re * re + im * im)
        power_ref[0, span] = high
        power_ref[1, span] = low
    pulse_mask = pulse_ref[...]
    high, low = split(dot(pulse_mask, power_ref[0]) + dot(pulse_mask, power_ref[1]))
    range_mask = range_ref[...]
    sums = dot_nt(range_mask, high) + dot_nt(range_mask, low)

    @pl.when(pl.program_id(0) == 0)
    def _():
        sums_ref[...] = sums

    @pl.when(pl.program_id(0) > 0)
    def _():
        sums_ref[...] += sums


def per_device(
    echoes, range_replica, azimuth_replicas, replica_index, azimuth_extent, range_extent
):
    count = lax.axis_size("row")
    device = lax.axis_index("row")
    me = device.astype(jnp.int32)[None]
    rows, _, samples = echoes.shape
    pulses = rows * count
    width = samples // count
    part = pulses // RADIX
    replicas = azimuth_replicas.shape[0]

    offsets = send_order(count) + [0]
    pieces = compress(me, echoes, range_replica, offsets, width)
    received = []
    for offset, piece in zip(offsets, pieces):
        if offset:
            piece = lax.ppermute(piece, "row", [(i, i ^ offset) for i in range(count)])
        received.append(piece)

    forward, inverse = (jnp.asarray(m) for m in phase_matrices(pulses))
    taps = jnp.transpose(azimuth_replicas, (1, 2, 0))
    chosen = pl.pallas_call(
        spectra_kernel,
        out_shape=jax.ShapeDtypeStruct((RADIX, 2 * part, width), F32),
        compiler_params=pltpu.CompilerParams(vmem_limit_bytes=VMEM_LIMIT),
        cost_estimate=pl.CostEstimate(flops=4 << 30, bytes_accessed=12 << 20, transcendentals=0),
        name="replica_spectra",
    )(taps, replica_index[None, :], forward)

    pulse_tiles = pulses // TILE
    pulse_start = jnp.arange(pulse_tiles, dtype=jnp.int32) * TILE - azimuth_extent
    pulse_stop = pulse_start + TILE + 2 * azimuth_extent
    at = jnp.arange(pulses, dtype=jnp.int32)[None, :]
    pulse_mask = ((at >= pulse_start[:, None]) & (at < pulse_stop[:, None])).astype(BF16)
    pulse_count = jnp.minimum(pulse_stop, pulses) - jnp.maximum(pulse_start, 0)

    tiles = width // TILE
    mask_rows = -(-(tiles + 2) // 16) * 16
    place = jnp.arange(mask_rows, dtype=jnp.int32)
    tile = device * tiles + jnp.where(place == tiles, -1, jnp.where(place == tiles + 1, tiles, place))
    exists = (place < tiles + 2) & (tile >= 0) & (tile < tiles * count)
    extent = range_extent[jnp.clip(tile, 0, tiles * count - 1)]
    range_start = tile * TILE - extent
    range_stop = range_start + TILE + 2 * extent
    at = device * width + jnp.arange(width, dtype=jnp.int32)[None, :]
    range_mask = (
        exists[:, None] & (at >= range_start[:, None]) & (at < range_stop[:, None])
    ).astype(BF16)
    range_count = (jnp.minimum(range_stop, samples) - jnp.maximum(range_start, 0))[:tiles]
    cells = (range_count[:, None] * pulse_count[None, :]).astype(F32)

    chunk = min(width, 256)
    steps = width // chunk
    whole = lambda shape: pl.BlockSpec(shape, lambda i: (0,) * len(shape), pipeline_mode=pl.Buffered(1))
    focused, sums = pl.pallas_call(
        functools.partial(azimuth_kernel, tuple(offsets)),
        grid=(steps,),
        out_shape=[
            jax.ShapeDtypeStruct((pulses, 2, width), BF16),
            jax.ShapeDtypeStruct((mask_rows, pulse_tiles), F32),
        ],
        in_specs=[
            pl.BlockSpec(memory_space=pltpu.SMEM),
            whole((2, RADIX, 2 * part, 2 * part)),
            whole((2, RADIX, 2 * part, 2 * part)),
            pl.BlockSpec((RADIX, 2 * part, chunk), lambda i: (0, 0, i)),
            whole((pulse_tiles, pulses)),
            pl.BlockSpec((mask_rows, chunk), lambda i: (0, i)),
        ]
        + [pl.BlockSpec((2, rows, chunk), lambda i: (0, 0, i))] * count,
        out_specs=[
            pl.BlockSpec((pulses, 2, chunk), lambda i: (0, 0, i)),
            pl.BlockSpec((mask_rows, pulse_tiles), lambda i: (0, 0)),
        ],
        scratch_shapes=[
            pltpu.VMEM((2, pulses, chunk), BF16),
            pltpu.VMEM((RADIX, 2 * part, chunk), F32),
            pltpu.VMEM((2, pulses, chunk), BF16),
        ],
        compiler_params=pltpu.CompilerParams(vmem_limit_bytes=VMEM_LIMIT),
        name="azimuth_focus",
    )(me, forward, inverse, chosen, pulse_mask, range_mask, *received)

    to_left = lax.ppermute(sums[tiles : tiles + 1], "row", [(i, i - 1) for i in range(1, count)])
    to_right = lax.ppermute(sums[tiles + 1 : tiles + 2], "row", [(i, i + 1) for i in range(count - 1)])
    pad = jnp.zeros((tiles - 2, pulse_tiles), F32)
    edges = jnp.concatenate([to_right, pad, to_left], axis=0)
    looked = (sums[:tiles] + edges) / cells
    return focused, looked


def solution(mesh):
    return jax.shard_map(
        per_device,
        mesh=mesh,
        in_specs=(
            P(("scene", "row"), None, None),
            P(),
            P(),
            P(("scene", "row")),
            P("scene"),
            P("scene"),
        ),
        out_specs=(P("scene", None, "row"), P(("scene", "row"), None)),
        check_vma=False,
    )
```

```python
import functools

import jax
import jax.numpy as jnp
import ml_dtypes
import numpy as np
from jax import lax
from jax.experimental import pallas as pl
from jax.experimental.pallas import tpu as pltpu
from jax.sharding import PartitionSpec as P

TILE = 16
RADIX = 4
CELL = 128
F32 = jnp.float32
BF16 = jnp.bfloat16
RANGE_VMEM = 24 << 20
FOCUS_VMEM = 24 << 20


def dot(a, b):
    return jnp.dot(a, b, preferred_element_type=F32)


def dot_nt(a, b):
    return lax.dot_general(a, b, (((1,), (1,)), ((), ())), preferred_element_type=F32)


def split(x):
    high = x.astype(BF16)
    low = (x - high.astype(F32)).astype(BF16)
    return high, low


def twice(x):
    return jnp.concatenate([x, x], axis=0)


def two_terms(matrix):
    high = matrix.astype(ml_dtypes.bfloat16)
    low = (matrix - high.astype(np.float64)).astype(ml_dtypes.bfloat16)
    return np.concatenate([high, low], axis=2)


@functools.lru_cache(maxsize=None)
def phase_matrices(length):
    part = length // RADIX
    index = np.arange(part)
    k = index.reshape(part // RADIX, RADIX).T.reshape(-1)
    step = np.arange(RADIX)[:, None, None]
    phase = (k[None, :, None] * (RADIX * index[None, None, :] + step)) % length
    angle = phase * (-2.0 * np.pi / length)
    forward = two_terms(np.concatenate([np.cos(angle), np.sin(angle)], axis=1))
    phase = (index[None, :, None] * (RADIX * index[None, None, :] + step)) % length
    angle = phase * (2.0 * np.pi / length)
    inverse = two_terms(np.concatenate([np.cos(angle), np.sin(angle)], axis=1))
    return forward, inverse


def complex_product(matrix, x):
    product = dot(matrix, twice(x))
    rows, lanes = product.shape[0] // 2, product.shape[1] // 2
    real = product[:rows, :lanes] - product[rows:, lanes:]
    imag = product[:rows, lanes:] + product[rows:, :lanes]
    return real, imag


def butterfly(x, sign):
    (ar, ai), (br, bi), (cr, ci), (dr, di) = x
    pr, pi, mr, mi = ar + cr, ai + ci, ar - cr, ai - ci
    sr, si, tr, ti = br + dr, bi + di, br - dr, bi - di
    if sign < 0:
        tr, ti = ti, -tr
    else:
        tr, ti = -ti, tr
    return [(pr + sr, pi + si), (mr + tr, mi + ti), (pr - sr, pi - si), (mr - tr, mi - ti)]


def spectrum_part(values, r):
    rows = values[0][0].shape[0] // RADIX
    span = slice(r * rows, (r + 1) * rows)
    parts = butterfly([(re[span], im[span]) for re, im in values], -1)
    return [jnp.concatenate([p[c] for p in parts], axis=0) for c in range(2)]


def table_kernel(h_ref, table):
    block = table.shape[1]
    taps = h_ref.shape[1]
    replica = h_ref[...].astype(F32)
    for part in range(2):
        line = jnp.concatenate([replica[part : part + 1], jnp.zeros((1, block), F32)], axis=1)
        lines = jnp.broadcast_to(line, (block, taps + block))
        table[part] = pltpu.roll(lines, 0, 1, stride=1, stride_axis=0).astype(BF16)


def windows(x_refs, base, width, blocks, count):
    pieces = []
    for step in range(blocks):
        place = base + step
        start = pl.multiple_of(jnp.minimum(place, count - 1) * width, width)
        pieces.append([x_ref.at[:, :, pl.ds(start, width)] for x_ref in x_refs])
    return pieces


def pulse_order(total, swapped):
    row = lax.broadcasted_iota(jnp.int32, (2 * total, 2 * total), 0)
    column = lax.broadcasted_iota(jnp.int32, (2 * total, 2 * total), 1)
    quarter = total // RADIX
    pulse = RADIX * (row % quarter) + (row % total) // quarter
    source = 2 * pulse + row // total
    source = jnp.where(swapped, (source + total) % (2 * total), source)
    return (column == source).astype(F32).astype(BF16)


def correlate(window, table, width, early_out, late_out):
    block = table.shape[1]
    taps = table.shape[2] - block
    total = window.shape[0] // 2
    stacked = jnp.concatenate(
        [window[:, j * block : j * block + block + taps] for j in range(width // block)], axis=0
    )
    with_real = dot_nt(stacked, table[0])
    with_imag = dot_nt(stacked, table[1])
    placed = [0, 0]
    for cell in range(width // CELL):
        at = 2 * total * (cell * CELL // block)
        re, im = slice(at, at + total), slice(at + total, at + 2 * total)
        lanes = slice(cell * CELL % block, cell * CELL % block + CELL)
        real = with_real[re, lanes] + with_imag[im, lanes]
        imag = with_real[im, lanes] - with_imag[re, lanes]
        late = late_out is not None and cell in LATE
        out = late_out if late else early_out
        place = placed[late]
        placed[late] += 1
        out[:, 2 * CELL * place : 2 * CELL * (place + 1)] = jnp.concatenate(
            [real.astype(BF16), imag.astype(BF16)], axis=1
        )


def first_range_kernel(offsets, width, me_ref, x_hbm, h_ref, *refs):
    outs, table, x_ref, sems = refs[:-3], refs[-3], refs[-2], refs[-1]
    rows = x_hbm.shape[0]
    count = x_hbm.shape[2] // width
    blocks = x_ref.shape[0]
    me = me_ref[0]
    base = me ^ offsets[0]
    base = base - base % 2
    copies = []
    for step, (piece,) in enumerate(windows([x_hbm], base, width, blocks, count)):
        copies.append(pltpu.make_async_copy(piece, x_ref.at[step], sems.at[step]))
    for copy in copies:
        copy.start()
    table_kernel(h_ref, table)
    order = pulse_order(rows, False)
    for copy in copies:
        copy.wait()
    pieces = []
    for step in range(blocks):
        piece = x_ref[step].reshape(2 * rows, width)
        pieces.append(jnp.where(base + step < count, piece, jnp.zeros_like(piece)))
    window = dot(order, jnp.concatenate(pieces, axis=1)).astype(BF16)
    reach = window.shape[1] - width
    for offset, out in zip(offsets, outs):
        odd = (me ^ offset) % 2
        mine = jnp.where(odd == 0, window[:, :reach], window[:, width:])
        correlate(mine, table, width, out, None)


def range_kernel(offsets, late, width, me_ref, x_ref, sibling_ref, table, after_ref, *outs):
    del after_ref
    rows = x_ref.shape[0]
    taps = table.shape[2] - table.shape[1]
    count = x_ref.shape[2] // width
    me = me_ref[0]
    order = pulse_order(2 * rows, me % 2 == 1)
    outs = iter(outs)
    for offset in offsets:
        owner = me ^ offset
        pieces = []
        for step, piece in enumerate(
            windows([x_ref, sibling_ref], owner, width, 1 + -(-taps // width), count)
        ):
            piece = jnp.concatenate([part[...].reshape(2 * rows, width) for part in piece], axis=0)
            if step:
                piece = jnp.where(owner + step < count, piece, jnp.zeros_like(piece))
            pieces.append(piece)
        window = dot(order, jnp.concatenate(pieces, axis=1)).astype(BF16)
        early_out = next(outs)
        late_out = next(outs) if offset in late else None
        correlate(window, table, width, early_out, late_out)


LATE = (1, 2)


def range_cost(offsets, total, width, taps):
    return pl.CostEstimate(
        flops=len(offsets) * 16 * total * width * (taps + 256),
        bytes_accessed=len(offsets) * 4 * total * width * 3,
        transcendentals=0,
    )


def compress_first(me, echoes, replica, offsets, width):
    rows = echoes.shape[0]
    block = min(256, width)
    taps = replica.shape[1]
    blocks = 2 + -(-taps // width)
    vmem = pl.BlockSpec(memory_space=pltpu.VMEM)
    outs = pl.pallas_call(
        functools.partial(first_range_kernel, tuple(offsets), width),
        out_shape=[jax.ShapeDtypeStruct((rows, 2 * width), BF16)] * len(offsets)
        + [jax.ShapeDtypeStruct((2, block, taps + block), BF16)],
        in_specs=[pl.BlockSpec(memory_space=pltpu.SMEM), pl.BlockSpec(memory_space=pl.ANY), vmem],
        out_specs=[vmem] * (len(offsets) + 1),
        scratch_shapes=[pltpu.VMEM((blocks, rows, 2, width), BF16), pltpu.SemaphoreType.DMA((blocks,))],
        compiler_params=pltpu.CompilerParams(vmem_limit_bytes=RANGE_VMEM),
        cost_estimate=range_cost(offsets, rows, width, taps),
        name="range_compress_first",
    )(me, echoes, replica)
    return dict(zip(offsets, outs)), outs[-1]


def compress(me, echoes, sibling, table, after, offsets, late, width):
    total = 2 * echoes.shape[0]
    vmem = pl.BlockSpec(memory_space=pltpu.VMEM)
    shapes = []
    for offset in offsets:
        if offset in late:
            shapes += [(total, 2 * (width - len(LATE) * CELL)), (total, 2 * len(LATE) * CELL)]
        else:
            shapes += [(total, 2 * width)]
    outs = pl.pallas_call(
        functools.partial(range_kernel, tuple(offsets), late, width),
        out_shape=[jax.ShapeDtypeStruct(shape, BF16) for shape in shapes],
        in_specs=[pl.BlockSpec(memory_space=pltpu.SMEM), vmem, vmem, vmem, pl.BlockSpec(memory_space=pl.ANY)],
        out_specs=[vmem] * len(shapes),
        compiler_params=pltpu.CompilerParams(vmem_limit_bytes=RANGE_VMEM),
        cost_estimate=range_cost(offsets, total, width, table.shape[2] - table.shape[1]),
        name="range_compress",
    )(me, echoes, sibling, table, after)
    outs = iter(outs)
    return {offset: (next(outs), next(outs) if offset in late else None) for offset in offsets}


def column(line, select):
    return jnp.sum(jnp.where(select, line, 0.0), axis=1, keepdims=True)


def tables_kernel(
    me_ref, taps_ref, azimuth_ref, range_ref, matrix_ref, after_ref,
    spectra_ref, pulse_ref, mask_ref, inside_ref,
):
    del after_ref
    part = matrix_ref.shape[1] // 2
    length = part * RADIX
    replicas, _, tap_count = taps_ref.shape
    row = lax.broadcasted_iota(jnp.int32, (2 * CELL, 2 * replicas), 0)
    source = lax.broadcasted_iota(jnp.int32, (2 * CELL, 2 * replicas), 1)
    place = (row % CELL < replicas) & (source == 2 * (row % CELL) + row // CELL)
    taps = taps_ref[...].reshape(2 * replicas, tap_count)
    taps = dot(place.astype(F32).astype(BF16), taps).astype(BF16)
    m = lax.broadcasted_iota(jnp.int32, (part, tap_count), 0)
    tap = lax.broadcasted_iota(jnp.int32, (part, tap_count), 1)
    values = []
    for q in range(RADIX):
        pick = (tap == RADIX * m + q).astype(F32).astype(BF16)
        values.append(complex_product(matrix_ref[q], dot_nt(pick, taps).astype(BF16)))
    for r in range(RADIX):
        spectrum = jnp.concatenate(spectrum_part(values, r), axis=0) * (1.0 / length)
        high, low = split(spectrum)
        spectra_ref[r] = jnp.concatenate([high[:, :replicas], low[:, :replicas]], axis=1)

    def mask(starts, stops, first, shape):
        at = (first + lax.broadcasted_iota(jnp.int32, shape, 1)).astype(F32)
        return ((at >= starts) & (at < stops)).astype(F32).astype(BF16)

    pulse_tiles = azimuth_ref.shape[1]
    extents = azimuth_ref[...].astype(F32)
    row = lax.broadcasted_iota(jnp.int32, (pulse_tiles, pulse_tiles), 0)
    lane = lax.broadcasted_iota(jnp.int32, (pulse_tiles, pulse_tiles), 1)
    extent = column(extents, row == lane)
    start = (TILE * lax.broadcasted_iota(jnp.int32, (pulse_tiles, 1), 0)).astype(F32)
    pulse_ref[...] = mask(start - extent, start + TILE + extent, 0, pulse_ref.shape)
    start = (TILE * lax.broadcasted_iota(jnp.int32, (1, pulse_tiles), 1)).astype(F32)
    pulse_count = jnp.minimum(start + TILE + extents, 1.0 * length) - jnp.maximum(start - extents, 0.0)

    tiles = inside_ref.shape[0]
    mask_rows, width = mask_ref.shape
    total = range_ref.shape[1]
    row = lax.broadcasted_iota(jnp.int32, (mask_rows, 1), 0)
    tile = me_ref[0] * tiles + jnp.where(row == tiles, -1, jnp.where(row == tiles + 1, tiles, row))
    exists = (row < tiles + 2) & (tile >= 0) & (tile < total)
    lane = lax.broadcasted_iota(jnp.int32, (mask_rows, total), 1)
    extent = column(range_ref[...].astype(F32), lane == tile)
    start = (TILE * tile).astype(F32) - extent
    stop = (TILE * tile + TILE).astype(F32) + extent
    mask_ref[...] = mask(start, jnp.where(exists, stop, start), me_ref[0] * width, mask_ref.shape)
    count = jnp.minimum(stop, 1.0 * TILE * total) - jnp.maximum(start, 0.0)
    inside_ref[...] = count[:tiles] * pulse_count


def make_tables(me, azimuth_replicas, azimuth_extent, range_extent, matrix, after, width):
    part = matrix.shape[1] // 2
    replicas = azimuth_replicas.shape[0]
    pulse_tiles = azimuth_extent.shape[0]
    tiles = width // TILE
    mask_rows = -(-(tiles + 2) // 16) * 16
    vmem = pl.BlockSpec(memory_space=pltpu.VMEM)
    shapes = [
        ((RADIX, 2 * part, 2 * replicas), BF16),
        ((pulse_tiles, RADIX * part), BF16),
        ((mask_rows, width), BF16),
        ((tiles, pulse_tiles), F32),
    ]
    return pl.pallas_call(
        tables_kernel,
        out_shape=[jax.ShapeDtypeStruct(*shape) for shape in shapes],
        in_specs=[pl.BlockSpec(memory_space=pltpu.SMEM)] + [vmem] * 4 + [pl.BlockSpec(memory_space=pl.ANY)],
        out_specs=[vmem] * 4,
        compiler_params=pltpu.CompilerParams(vmem_limit_bytes=RANGE_VMEM),
        cost_estimate=pl.CostEstimate(flops=1 << 31, bytes_accessed=4 << 20, transcendentals=0),
        name="tables",
    )(me, azimuth_replicas, azimuth_extent[None, :], range_extent[None, :], matrix, after)


def focus_kernel(
    offsets, places, cells, first, me_ref, forward_ref, inverse_ref, spectra_ref, index_ref, pulse_ref, range_ref, *refs
):
    sources, refs = refs[: len(offsets)], refs[len(offsets) :]
    if first:
        focused_ref, sums_ref, left_ref, right_ref, x_ref, v_ref, w_ref, power_ref = refs
        tiles = sums_ref.shape[0]
    else:
        _, early_ref, from_left_ref, from_right_ref, inside_ref = refs[:5]
        focused_ref, looked_ref, x_ref, v_ref, w_ref, power_ref = refs[5:]
        tiles = looked_ref.shape[0]
    total = max(source.shape[0] for source in sources)
    length = focused_ref.shape[0]
    part = length // RADIX
    quarter = total // RADIX
    direct = x_ref.shape[0] == RADIX
    me = me_ref[0]
    step = pl.program_id(0)

    def lanes_of(values, size):
        place = values[0]
        for n in range(1, len(values)):
            place = jnp.where(step == n, values[n], place)
        return pl.ds(pl.multiple_of(place * size, size), size)

    cell = lanes_of(cells, CELL)
    for offset, source in zip(offsets, sources):
        at = lanes_of(places[offset], 2 * CELL)
        rows = source.shape[0]
        owner = (me ^ offset) // (2 * rows // total)
        rows = rows // RADIX if direct else rows
        start = pl.multiple_of(owner * rows, rows)
        if direct:
            for q in range(RADIX):
                x_ref[q, pl.ds(start, rows), :] = source[q * rows : (q + 1) * rows, at]
        else:
            x_ref[pl.ds(start, rows), :] = source[:, at]
    for q in range(RADIX):
        if direct:
            x = x_ref[q]
        else:
            m = lax.broadcasted_iota(jnp.int32, (part, length), 0)
            column = lax.broadcasted_iota(jnp.int32, (part, length), 1)
            pick = column == (m // quarter) * total + q * quarter + m % quarter
            x = dot(pick.astype(F32).astype(BF16), x_ref[...]).astype(BF16)
        v_ref[q, 0], v_ref[q, 1] = complex_product(forward_ref[q], x)
    replicas = spectra_ref.shape[2] // 2
    row = lax.broadcasted_iota(jnp.int32, (2 * replicas, CELL), 0)
    chosen = (row % replicas == index_ref[:, cell]).astype(F32).astype(BF16)
    for r in range(RADIX):
        sr, si = spectrum_part([(v_ref[q, 0], v_ref[q, 1]) for q in range(RADIX)], r)
        replica = dot(spectra_ref[r], chosen)
        gr, gi = replica[:part], replica[part:]
        y = jnp.concatenate([sr * gr + si * gi, si * gr - sr * gi], axis=1).astype(BF16)
        w_ref[r, 0], w_ref[r, 1] = complex_product(inverse_ref[r], y)
    w = [(w_ref[r, 0], w_ref[r, 1]) for r in range(RADIX)]
    for q, (re, im) in enumerate(butterfly(w, 1)):
        span = slice(q * part, (q + 1) * part)
        both = jnp.stack([re.astype(BF16), im.astype(BF16)], axis=0)
        focused_ref[span] = jnp.swapaxes(both, 0, 1)
        power_ref[span] = jnp.concatenate(split(re * re + im * im), axis=1)
    sums = dot(pulse_ref[...], power_ref[...])
    high, low = split(sums[:, :CELL] + sums[:, CELL:])
    range_mask = range_ref[:, cell]
    sums = dot_nt(
        jnp.concatenate([range_mask, range_mask], axis=1), jnp.concatenate([high, low], axis=1)
    )
    if first:

        @pl.when(step == 0)
        def _():
            sums_ref[...] = sums[:tiles]
            left_ref[...] = sums[tiles : tiles + 1]
            right_ref[...] = sums[tiles + 1 : tiles + 2]

        @pl.when(step > 0)
        def _():
            sums_ref[...] += sums[:tiles]
            left_ref[...] += sums[tiles : tiles + 1]
            right_ref[...] += sums[tiles + 1 : tiles + 2]

    else:

        @pl.when(step == 0)
        def _():
            row = lax.broadcasted_iota(jnp.int32, looked_ref.shape, 0)
            looked_ref[...] = (
                early_ref[...]
                + sums[:tiles]
                + jnp.where(row == 0, from_left_ref[...], 0.0)
                + jnp.where(row == tiles - 1, from_right_ref[...], 0.0)
            )

        @pl.when(step > 0)
        def _():
            looked_ref[...] += sums[:tiles]

        @pl.when(step == len(cells) - 1)
        def _():
            looked_ref[...] /= inside_ref[...]


def focus(first, cells, places, pulses, width, tiles, tables, sources, more):
    me, forward, inverse, spectra, index, pulse_mask, range_mask = tables
    pulse_tiles = pulse_mask.shape[0]
    part = pulses // RADIX
    offsets = list(sources)

    def cell_of(step):
        place = cells[0]
        for n in range(1, len(cells)):
            place = jnp.where(step == n, cells[n], place)
        return place

    def whole(shape):
        return pl.BlockSpec(shape, lambda i: (0,) * len(shape))

    vmem = pl.BlockSpec(memory_space=pltpu.VMEM)
    in_specs = [pl.BlockSpec(memory_space=pltpu.SMEM)] + [vmem] * (6 + len(offsets))
    focused_shape = jax.ShapeDtypeStruct((pulses, 2, width), BF16)
    focused_spec = pl.BlockSpec((pulses, 2, CELL), lambda i: (0, 0, cell_of(i)))
    looks = (tiles, pulse_tiles)
    edge = (1, pulse_tiles)
    if first:
        out_shape = [focused_shape] + [jax.ShapeDtypeStruct(s, F32) for s in (looks, edge, edge)]
        out_specs = [focused_spec, whole(looks), whole(edge), whole(edge)]
        aliases = {}
    else:
        in_specs += [pl.BlockSpec(memory_space=pl.ANY)] + [vmem] * 4
        out_shape = [focused_shape, jax.ShapeDtypeStruct(looks, F32)]
        out_specs = [focused_spec, whole(looks)]
        aliases = {7 + len(offsets): 0}
    direct = all(source.shape[0] % (16 * RADIX) == 0 for source in sources.values())
    x_shape = (RADIX, part, 2 * CELL) if direct else (pulses, 2 * CELL)
    return pl.pallas_call(
        functools.partial(focus_kernel, tuple(offsets), places, tuple(cells), first),
        grid=(len(cells),),
        out_shape=out_shape,
        in_specs=in_specs,
        out_specs=out_specs,
        scratch_shapes=[
            pltpu.VMEM(x_shape, BF16),
            pltpu.VMEM((RADIX, 2, part, CELL), F32),
            pltpu.VMEM((RADIX, 2, part, CELL), F32),
            pltpu.VMEM((pulses, 2 * CELL), BF16),
        ],
        input_output_aliases=aliases,
        compiler_params=pltpu.CompilerParams(vmem_limit_bytes=FOCUS_VMEM),
        cost_estimate=pl.CostEstimate(
            flops=len(cells) << 31, bytes_accessed=len(cells) << 21, transcendentals=0
        ),
        name="azimuth_focus",
    )(me, forward, inverse, spectra, index, pulse_mask, range_mask, *sources.values(), *more)


def per_device(
    echoes, range_replica, azimuth_replicas, replica_index, azimuth_extent, range_extent
):
    count = lax.axis_size("row")
    device = lax.axis_index("row")
    me = device.astype(jnp.int32)[None]
    rows, _, samples = echoes.shape
    pulses = rows * count
    width = samples // count
    cells = list(range(width // CELL))
    chunked = len(cells) == RADIX

    def send(piece, offset):
        if offset == 0:
            return piece
        return lax.ppermute(piece, "row", [(i, i ^ offset) for i in range(count)])

    sibling = send(echoes, 1)
    far = list(range(count // 2, count, 2))
    near = list(range(2, count // 2, 2))
    alone = [far[0], far[0] + 1] if chunked else [0]
    if chunked:
        far = far[1:]
    late = frozenset(far) if chunked else frozenset()
    half = len(far) // 2
    far = far[half:] + far[:half]
    near = near[half:] + near[:half]
    alone, table = compress_first(me, echoes, range_replica, alone, width)
    after = table
    pieces = {}
    if chunked:
        pieces = {offset: (piece, None) for offset, piece in alone.items()}
        pieces.update(compress(me, echoes, sibling, table, after, far[:1], late, width))
        after = pieces[far[0]][1]
        far = far[1:]
    rest = []
    while near or far:
        rest += far[:1] + near[:1]
        near, far = near[1:], far[1:]
    pieces.update(compress(me, echoes, sibling, table, after, rest + [0], late, width))
    received = {offset: send(piece, offset) for offset, (piece, _) in pieces.items()}
    received_late = {offset: send(pieces[offset][1], offset) for offset in pieces if offset in late}

    forward, inverse = (jnp.asarray(m) for m in phase_matrices(pulses))
    tiles = width // TILE
    spectra, pulse_mask, range_mask, inside = make_tables(
        me, azimuth_replicas, azimuth_extent, range_extent, forward, pieces[0][0], width
    )
    tables = (me, forward, inverse, spectra, replica_index[None, :], pulse_mask, range_mask)
    early = [cell for cell in cells if not (chunked and cell in LATE)]
    places = {offset: list(range(len(early))) if offset in late else early for offset in received}
    focused, sums, left, right = focus(
        True, early, places, pulses, width, tiles, tables, received, ()
    )
    from_right = lax.ppermute(left, "row", [(i, i - 1) for i in range(1, count)])
    from_left = lax.ppermute(right, "row", [(i, i + 1) for i in range(count - 1)])
    if not chunked:
        pad = jnp.zeros((tiles - 2, sums.shape[1]), F32)
        edges = jnp.concatenate([from_left, pad, from_right], axis=0)
        return focused, (sums + edges) / inside
    places = {offset: list(range(len(LATE))) if offset in late else LATE for offset in received}
    sources = {offset: received_late.get(offset, received[offset]) for offset in received}
    more = (focused, sums, from_left, from_right, inside)
    focused, looked = focus(
        False, LATE, places, pulses, width, tiles, tables, sources, more
    )
    return focused, looked


def solution(mesh):
    return jax.shard_map(
        per_device,
        mesh=mesh,
        in_specs=(
            P(("scene", "row"), None, None),
            P(),
            P(),
            P(("scene", "row")),
            P("scene"),
            P("scene"),
        ),
        out_specs=(P("scene", None, "row"), P(("scene", "row"), None)),
        check_vma=False,
    )
```

```python
import functools

import jax
import jax.numpy as jnp
import ml_dtypes
import numpy as np
from jax import lax
from jax.experimental import pallas as pl
from jax.experimental.pallas import tpu as pltpu
from jax.sharding import PartitionSpec as P

TILE = 16
RADIX = 4
CELL = 128
F32 = jnp.float32
BF16 = jnp.bfloat16
FIRST_VMEM = 24 << 20
RANGE_VMEM = 24 << 20
GATE_VMEM = 1 << 20
FOCUS_VMEM = 24 << 20
SMALL_COST = pl.CostEstimate(flops=1 << 20, bytes_accessed=1 << 16, transcendentals=0)


def dot(a, b):
    return jnp.dot(a, b, preferred_element_type=F32)


def dot_nt(a, b):
    return lax.dot_general(a, b, (((1,), (1,)), ((), ())), preferred_element_type=F32)


def split(x):
    high = x.astype(BF16)
    low = (x - high.astype(F32)).astype(BF16)
    return high, low


def twice(x):
    return jnp.concatenate([x, x], axis=0)


def two_terms(matrix):
    high = matrix.astype(ml_dtypes.bfloat16)
    low = (matrix - high.astype(np.float64)).astype(ml_dtypes.bfloat16)
    return np.concatenate([high, low], axis=2)


@functools.lru_cache(maxsize=None)
def phase_matrices(length):
    part = length // RADIX
    index = np.arange(part)
    k = index.reshape(part // RADIX, RADIX).T.reshape(-1)
    step = np.arange(RADIX)[:, None, None]
    phase = (k[None, :, None] * (RADIX * index[None, None, :] + step)) % length
    angle = phase * (2.0 * np.pi / length)
    cos, sin = np.cos(angle), np.sin(angle)
    forward = two_terms(np.concatenate([cos, -sin], axis=1))
    inverse = two_terms(np.concatenate([cos, sin], axis=2).reshape(RADIX, part, 2, part).transpose(0, 2, 3, 1).reshape(RADIX, 2 * part, part))
    return forward, inverse


def complex_product(matrix, x):
    product = dot(matrix, twice(x))
    rows, lanes = product.shape[0] // 2, product.shape[1] // 2
    real = product[:rows, :lanes] - product[rows:, lanes:]
    imag = product[:rows, lanes:] + product[rows:, :lanes]
    return real, imag


def butterfly(x, sign):
    (ar, ai), (br, bi), (cr, ci), (dr, di) = x
    pr, pi, mr, mi = ar + cr, ai + ci, ar - cr, ai - ci
    sr, si, tr, ti = br + dr, bi + di, br - dr, bi - di
    if sign < 0:
        tr, ti = ti, -tr
    else:
        tr, ti = -ti, tr
    return [(pr + sr, pi + si), (mr + tr, mi + ti), (pr - sr, pi - si), (mr - tr, mi - ti)]


def spectrum_part(values, r):
    rows = values[0][0].shape[0] // RADIX
    span = slice(r * rows, (r + 1) * rows)
    parts = butterfly([(re[span], im[span]) for re, im in values], -1)
    return [jnp.concatenate([p[c] for p in parts], axis=0) for c in range(2)]


def table_kernel(h_ref, table):
    block = table.shape[1]
    for part in range(2):
        lines = jnp.broadcast_to(h_ref[part : part + 1], (block, h_ref.shape[1]))
        table[part] = pltpu.roll(lines, 0, 1, stride=1, stride_axis=0).astype(BF16)


def windows(x_refs, base, width, blocks, count):
    pieces = []
    for step in range(blocks):
        place = base + step
        start = pl.multiple_of(jnp.minimum(place, count - 1) * width, width)
        pieces.append([x_ref.at[:, :, pl.ds(start, width)] for x_ref in x_refs])
    return pieces


def pulse_order(total, swapped):
    row = lax.broadcasted_iota(jnp.int32, (2 * total, 2 * total), 0)
    column = lax.broadcasted_iota(jnp.int32, (2 * total, 2 * total), 1)
    quarter = total // RADIX
    pulse = RADIX * (row % quarter) + (row % total) // quarter
    source = 2 * pulse + row // total
    source = jnp.where(swapped, (source + total) % (2 * total), source)
    return (column == source).astype(F32).astype(BF16)


def correlate(window, table, width, early_out, late_out):
    block = table.shape[1]
    taps = table.shape[2] - block
    total = window.shape[0] // 2
    stacked = jnp.concatenate(
        [window[:, j * block : j * block + block + taps] for j in range(width // block)], axis=0
    )
    with_real = dot_nt(stacked, table[0])
    with_imag = dot_nt(stacked, table[1])
    placed = [0, 0]
    for cell in range(width // CELL):
        at = 2 * total * (cell * CELL // block)
        re, im = slice(at, at + total), slice(at + total, at + 2 * total)
        lanes = slice(cell * CELL % block, cell * CELL % block + CELL)
        real = with_real[re, lanes] + with_imag[im, lanes]
        imag = with_real[im, lanes] - with_imag[re, lanes]
        late = late_out is not None and cell in LATE
        out = late_out if late else early_out
        place = placed[late]
        placed[late] += 1
        out[:, 2 * CELL * place : 2 * CELL * (place + 1)] = jnp.concatenate(
            [real.astype(BF16), imag.astype(BF16)], axis=1
        )


def first_range_kernel(offsets, width, me_ref, x_hbm, h_ref, *refs):
    outs, (table, x_ref, sems) = refs[:-3], refs[-3:]
    rows = x_hbm.shape[0]
    count = x_hbm.shape[2] // width
    blocks = x_ref.shape[0]
    me = me_ref[0]
    base = me ^ offsets[0]
    base = base - base % 2
    copies = []
    for step, (piece,) in enumerate(windows([x_hbm], base, width, blocks, count)):
        copies.append(pltpu.make_async_copy(piece, x_ref.at[step], sems.at[step]))
    for copy in copies:
        copy.start()
    table_kernel(h_ref, table)
    order = pulse_order(rows, False)
    for copy in copies:
        copy.wait()
    pieces = []
    for step in range(blocks):
        piece = x_ref[step].reshape(2 * rows, width)
        pieces.append(jnp.where(base + step < count, piece, jnp.zeros_like(piece)))
    window = dot(order, jnp.concatenate(pieces, axis=1)).astype(BF16)
    reach = window.shape[1] - width
    for offset, out in zip(offsets, outs):
        odd = (me ^ offset) % 2
        mine = jnp.where(odd == 0, window[:, :reach], window[:, width:])
        correlate(mine, table, width, out, None)


def range_kernel(offsets, late, width, me_ref, x_ref, sibling_ref, h_ref, after_ref, *refs):
    del after_ref
    outs, table = refs[:-1], refs[-1]
    table_kernel(h_ref, table)
    rows = x_ref.shape[0]
    taps = table.shape[2] - table.shape[1]
    count = x_ref.shape[2] // width
    me = me_ref[0]
    order = pulse_order(2 * rows, me % 2 == 1)
    outs = iter(outs)
    for offset in offsets:
        owner = me ^ offset
        pieces = []
        for step, piece in enumerate(
            windows([x_ref, sibling_ref], owner, width, 1 + -(-taps // width), count)
        ):
            piece = jnp.concatenate([part[...].reshape(2 * rows, width) for part in piece], axis=0)
            if step:
                piece = jnp.where(owner + step < count, piece, jnp.zeros_like(piece))
            pieces.append(piece)
        window = dot(order, jnp.concatenate(pieces, axis=1)).astype(BF16)
        early_out = next(outs)
        late_out = next(outs) if offset in late else None
        correlate(window, table, width, early_out, late_out)


LATE = (1, 2)


def compress_first(me, echoes, replica, offsets, width):
    rows = echoes.shape[0]
    block = min(256, width)
    taps = replica.shape[1] - block
    blocks = 2 + -(-taps // width)
    vmem = pl.BlockSpec(memory_space=pltpu.VMEM)
    outs = pl.pallas_call(
        functools.partial(first_range_kernel, tuple(offsets), width),
        out_shape=[jax.ShapeDtypeStruct((rows, 2 * width), BF16)] * len(offsets),
        in_specs=[pl.BlockSpec(memory_space=pltpu.SMEM), pl.BlockSpec(memory_space=pl.ANY), vmem],
        out_specs=[vmem] * len(offsets),
        scratch_shapes=[
            pltpu.VMEM((2, block, taps + block), BF16),
            pltpu.VMEM((blocks, rows, 2, width), BF16),
            pltpu.SemaphoreType.DMA((blocks,)),
        ],
        compiler_params=pltpu.CompilerParams(vmem_limit_bytes=FIRST_VMEM),
        cost_estimate=pl.CostEstimate(
            flops=len(offsets) * 16 * rows * width * (taps + 256),
            bytes_accessed=len(offsets) * 4 * rows * width * 3,
            transcendentals=0,
        ),
        name="range_compress_first",
    )(me, echoes, replica)
    return dict(zip(offsets, outs))


def compress(me, echoes, sibling, replica, after, offsets, late, width):
    total = 2 * echoes.shape[0]
    block = min(256, width)
    taps = replica.shape[1] - block
    vmem = pl.BlockSpec(memory_space=pltpu.VMEM)
    shapes = []
    for offset in offsets:
        if offset in late:
            shapes += [(total, 2 * (width - len(LATE) * CELL)), (total, 2 * len(LATE) * CELL)]
        else:
            shapes += [(total, 2 * width)]
    outs = pl.pallas_call(
        functools.partial(range_kernel, tuple(offsets), late, width),
        out_shape=[jax.ShapeDtypeStruct(shape, BF16) for shape in shapes],
        in_specs=[pl.BlockSpec(memory_space=pltpu.SMEM), vmem, vmem, vmem, pl.BlockSpec(memory_space=pl.ANY)],
        out_specs=[vmem] * len(shapes),
        scratch_shapes=[pltpu.VMEM((2, block, taps + block), BF16)],
        compiler_params=pltpu.CompilerParams(vmem_limit_bytes=RANGE_VMEM),
        cost_estimate=pl.CostEstimate(
            flops=len(offsets) * 16 * total * width * (taps + block),
            bytes_accessed=len(offsets) * 4 * total * width * 3,
            transcendentals=0,
        ),
        name="range_compress",
    )(me, echoes, sibling, replica, after)
    outs = iter(outs)
    return {offset: (next(outs), next(outs) if offset in late else None) for offset in offsets}


def gate_kernel(*refs):
    del refs


def gate(pieces, after):
    anywhere = pl.BlockSpec(memory_space=pl.ANY)
    return pl.pallas_call(
        gate_kernel,
        out_shape=[jax.ShapeDtypeStruct(piece.shape, piece.dtype) for piece in pieces],
        in_specs=[anywhere] * (len(pieces) + len(after)),
        out_specs=[anywhere] * len(pieces),
        input_output_aliases={n: n for n in range(len(pieces))},
        compiler_params=pltpu.CompilerParams(vmem_limit_bytes=GATE_VMEM),
        cost_estimate=SMALL_COST,
        name="gate",
    )(*pieces, *after)


def column(line, select):
    return jnp.sum(jnp.where(select, line, 0.0), axis=1, keepdims=True)


def tables_kernel(
    me_ref, taps_ref, azimuth_ref, range_ref, matrix_ref, after_ref,
    spectra_ref, pulse_ref, mask_ref, inside_ref,
):
    del after_ref
    part = matrix_ref.shape[1] // 2
    length = part * RADIX
    replicas, _, tap_count = taps_ref.shape
    row = lax.broadcasted_iota(jnp.int32, (2 * CELL, 2 * replicas), 0)
    source = lax.broadcasted_iota(jnp.int32, (2 * CELL, 2 * replicas), 1)
    place = (row % CELL < replicas) & (source == 2 * (row % CELL) + row // CELL)
    taps = taps_ref[...].reshape(2 * replicas, tap_count)
    taps = dot(place.astype(F32).astype(BF16), taps).astype(BF16)
    m = lax.broadcasted_iota(jnp.int32, (part, tap_count), 0)
    tap = lax.broadcasted_iota(jnp.int32, (part, tap_count), 1)
    values = []
    for q in range(RADIX):
        pick = (tap == RADIX * m + q).astype(F32).astype(BF16)
        values.append(complex_product(matrix_ref[q], dot_nt(pick, taps).astype(BF16)))
    for r in range(RADIX):
        spectrum = jnp.concatenate(spectrum_part(values, r), axis=0) * (1.0 / length)
        high, low = split(spectrum)
        spectra_ref[r] = jnp.concatenate([high[:, :replicas], low[:, :replicas]], axis=1)

    def mask(starts, stops, at):
        at = at.astype(F32)
        return ((at >= starts) & (at < stops)).astype(F32).astype(BF16)

    pulse_tiles = azimuth_ref.shape[1]
    extents = azimuth_ref[...].astype(F32)
    row = lax.broadcasted_iota(jnp.int32, (pulse_tiles, pulse_tiles), 0)
    lane = lax.broadcasted_iota(jnp.int32, (pulse_tiles, pulse_tiles), 1)
    extent = column(extents, row == lane)
    start = (TILE * lax.broadcasted_iota(jnp.int32, (pulse_tiles, 1), 0)).astype(F32)
    lane = lax.broadcasted_iota(jnp.int32, pulse_ref.shape, 1)
    pulse_ref[...] = mask(start - extent, start + TILE + extent, RADIX * (lane % part) + lane // part)
    start = (TILE * lax.broadcasted_iota(jnp.int32, (1, pulse_tiles), 1)).astype(F32)
    pulse_count = jnp.minimum(start + TILE + extents, 1.0 * length) - jnp.maximum(start - extents, 0.0)

    tiles = inside_ref.shape[0]
    mask_rows, width = mask_ref.shape
    total = range_ref.shape[1]
    row = lax.broadcasted_iota(jnp.int32, (mask_rows, 1), 0)
    tile = me_ref[0] * tiles + jnp.where(row == tiles, -1, jnp.where(row == tiles + 1, tiles, row))
    exists = (row < tiles + 2) & (tile >= 0) & (tile < total)
    lane = lax.broadcasted_iota(jnp.int32, (mask_rows, total), 1)
    extent = column(range_ref[...].astype(F32), lane == tile)
    start = (TILE * tile).astype(F32) - extent
    stop = (TILE * tile + TILE).astype(F32) + extent
    lane = lax.broadcasted_iota(jnp.int32, mask_ref.shape, 1)
    mask_ref[...] = mask(start, jnp.where(exists, stop, start), me_ref[0] * width + lane)
    count = jnp.minimum(stop, 1.0 * TILE * total) - jnp.maximum(start, 0.0)
    inside_ref[...] = count[:tiles] * pulse_count


def make_tables(me, azimuth_replicas, azimuth_extent, range_extent, matrix, after, width):
    part = matrix.shape[1] // 2
    replicas = azimuth_replicas.shape[0]
    pulse_tiles = azimuth_extent.shape[0]
    tiles = width // TILE
    mask_rows = -(-(tiles + 2) // 16) * 16
    vmem = pl.BlockSpec(memory_space=pltpu.VMEM)
    shapes = [
        ((RADIX, 2 * part, 2 * replicas), BF16),
        ((pulse_tiles, RADIX * part), BF16),
        ((mask_rows, width), BF16),
        ((tiles, pulse_tiles), F32),
    ]
    return pl.pallas_call(
        tables_kernel,
        out_shape=[jax.ShapeDtypeStruct(*shape) for shape in shapes],
        in_specs=[pl.BlockSpec(memory_space=pltpu.SMEM)] + [vmem] * 4 + [pl.BlockSpec(memory_space=pl.ANY)],
        out_specs=[vmem] * 4,
        compiler_params=pltpu.CompilerParams(vmem_limit_bytes=RANGE_VMEM),
        cost_estimate=pl.CostEstimate(flops=1 << 31, bytes_accessed=4 << 20, transcendentals=0),
        name="tables",
    )(me, azimuth_replicas, azimuth_extent[None, :], range_extent[None, :], matrix, after)


def gather_pulses(offsets, places, n, sources, me, total, x_ref):
    direct = x_ref.shape[0] == RADIX
    for offset, source in zip(offsets, sources):
        at = slice(2 * CELL * places[offset][n], 2 * CELL * (places[offset][n] + 1))
        rows = source.shape[0]
        owner = (me ^ offset) // (2 * rows // total)
        rows = rows // RADIX if direct else rows
        start = pl.multiple_of(owner * rows, rows)
        if direct:
            for q in range(RADIX):
                span = slice(q * rows, (q + 1) * rows)
                x_ref[q, pl.ds(start, rows), :] = source[span, at]
        else:
            x_ref[pl.ds(start, rows), :] = source[:, at]


def pulses_of(x_ref, q, total, part):
    if x_ref.shape[0] == RADIX:
        return x_ref[q]
    quarter = total // RADIX
    m = lax.broadcasted_iota(jnp.int32, (part, x_ref.shape[0]), 0)
    row = lax.broadcasted_iota(jnp.int32, (part, x_ref.shape[0]), 1)
    pick = row == (m // quarter) * total + q * quarter + m % quarter
    return dot(pick.astype(F32).astype(BF16), x_ref[...]).astype(BF16)


def focus_kernel(
    offsets, places, cells, first, me_ref, forward_ref, inverse_ref, spectra_ref, index_ref, pulse_ref, range_ref, *refs
):
    sources, refs = refs[: len(offsets)], refs[len(offsets) :]
    if first:
        focused_hbm, sums_ref, left_ref, right_ref = refs[:4]
        tiles = sums_ref.shape[0]
    else:
        _, early_ref, from_left_ref, from_right_ref, inside_ref, focused_hbm, looked_ref = refs[:7]
        tiles = looked_ref.shape[0]
    x_ref, v_ref, s_ref, power_ref, image_ref, sems = refs[-6:]
    total = max(source.shape[0] for source in sources)
    part = v_ref.shape[3]
    me = me_ref[0]
    steps = range(len(cells))
    for n in steps:
        gather_pulses(offsets, places, n, sources, me, total, x_ref.at[n])
    replicas = spectra_ref.shape[2] // 2
    row = lax.broadcasted_iota(jnp.int32, (2 * replicas, CELL), 0)

    def transform(n):
        for q in range(RADIX):
            x = pulses_of(x_ref.at[n], q, total, part)
            v_ref[n, q, 0], v_ref[n, q, 1] = complex_product(forward_ref[q], x)

    def correlate_cell(n):
        lanes = slice(cells[n] * CELL, (cells[n] + 1) * CELL)
        chosen = (row % replicas == index_ref[:, lanes]).astype(F32).astype(BF16)
        rows = part // RADIX
        for r in range(RADIX):
            span = slice(r * rows, (r + 1) * rows)
            x = butterfly([(v_ref[n, q, 0, span], v_ref[n, q, 1, span]) for q in range(RADIX)], -1)
            replica = dot(spectra_ref[r], chosen)
            y = []
            for j, (sr, si) in enumerate(x):
                gr = replica[j * rows : (j + 1) * rows]
                gi = replica[part + j * rows : part + (j + 1) * rows]
                y.append((sr * gr + si * gi, si * gr - sr * gi))
            for q, (re, im) in enumerate(butterfly(y, 1)):
                s_ref[n, q, span, :CELL] = re.astype(BF16)
                s_ref[n, q, span, CELL:] = im.astype(BF16)

    copies = []

    def finish(n):
        lanes = slice(cells[n] * CELL, (cells[n] + 1) * CELL)
        for q in range(RADIX):
            re, im = complex_product(inverse_ref[q], s_ref[n, q])
            both = jnp.stack([re.astype(BF16), im.astype(BF16)], axis=0)
            image_ref[n, q] = jnp.swapaxes(both, 0, 1)
            copy = pltpu.make_async_copy(
                image_ref.at[n, q], focused_hbm.at[:, q, :, lanes], sems.at[n, q]
            )
            copy.start()
            copies.append(copy)
            power = (re * re + im * im).astype(BF16)
            power_ref[q * part : (q + 1) * part, n * CELL : (n + 1) * CELL] = power

    for n in steps:
        transform(n)
    for n in steps:
        correlate_cell(n)
    for n in steps:
        finish(n)
    sums = dot(pulse_ref[...], power_ref[...])
    high, low = split(sums)
    mask = jnp.concatenate([range_ref[:, cell * CELL : (cell + 1) * CELL] for cell in cells], axis=1)
    sums = dot_nt(jnp.concatenate([mask, mask], axis=1), jnp.concatenate([high, low], axis=1))
    if first:
        sums_ref[...] = sums[:tiles]
        left_ref[...] = sums[tiles : tiles + 1]
        right_ref[...] = sums[tiles + 1 : tiles + 2]
    else:
        row = lax.broadcasted_iota(jnp.int32, looked_ref.shape, 0)
        looked_ref[...] = (
            early_ref[...]
            + sums[:tiles]
            + jnp.where(row == 0, from_left_ref[...], 0.0)
            + jnp.where(row == tiles - 1, from_right_ref[...], 0.0)
        ) / inside_ref[...]
    for copy in copies:
        copy.wait()


def focus(first, cells, places, pulses, width, tiles, tables, sources, more):
    me, forward, inverse, spectra, index, pulse_mask, range_mask = tables
    pulse_tiles = pulse_mask.shape[0]
    part = pulses // RADIX
    offsets = list(sources)
    vmem = pl.BlockSpec(memory_space=pltpu.VMEM)
    anywhere = pl.BlockSpec(memory_space=pl.ANY)
    in_specs = [pl.BlockSpec(memory_space=pltpu.SMEM)] + [vmem] * (6 + len(offsets))
    shapes = [jax.ShapeDtypeStruct((part, RADIX, 2, width), BF16)]
    shapes += [jax.ShapeDtypeStruct((tiles, pulse_tiles), F32)]
    if first:
        shapes += [jax.ShapeDtypeStruct((1, pulse_tiles), F32)] * 2
    else:
        in_specs += [anywhere] + [vmem] * 4
    direct = all(source.shape[0] % (16 * RADIX) == 0 for source in sources.values())
    x_shape = (RADIX, part, 2 * CELL) if direct else (pulses, 2 * CELL)
    return pl.pallas_call(
        functools.partial(focus_kernel, tuple(offsets), places, tuple(cells), first),
        out_shape=shapes,
        in_specs=in_specs,
        out_specs=[anywhere] + [vmem] * (len(shapes) - 1),
        scratch_shapes=[
            pltpu.VMEM((len(cells),) + x_shape, BF16),
            pltpu.VMEM((len(cells), RADIX, 2, part, CELL), F32),
            pltpu.VMEM((len(cells), RADIX, part, 2 * CELL), BF16),
            pltpu.VMEM((pulses, len(cells) * CELL), BF16),
            pltpu.VMEM((len(cells), RADIX, part, 2, CELL), BF16),
            pltpu.SemaphoreType.DMA((len(cells), RADIX)),
        ],
        input_output_aliases={} if first else {7 + len(offsets): 0},
        compiler_params=pltpu.CompilerParams(vmem_limit_bytes=FOCUS_VMEM),
        cost_estimate=pl.CostEstimate(
            flops=len(cells) << 31, bytes_accessed=len(cells) << 21, transcendentals=0
        ),
        name="azimuth_focus",
    )(me, forward, inverse, spectra, index, pulse_mask, range_mask, *sources.values(), *more)


def per_device(
    echoes, range_replica, azimuth_replicas, replica_index, azimuth_extent, range_extent
):
    count = lax.axis_size("row")
    device = lax.axis_index("row")
    me = device.astype(jnp.int32)[None]
    rows, _, samples = echoes.shape
    pulses = rows * count
    width = samples // count
    cells = list(range(width // CELL))
    chunked = len(cells) == RADIX and count == 16

    def send(piece, offset):
        if offset == 0:
            return piece
        return lax.ppermute(piece, "row", [(i, i ^ offset) for i in range(count)])

    sibling = send(echoes, 1)
    replica = jnp.pad(range_replica.astype(F32), ((0, 0), (0, min(256, width))))
    if chunked:
        late = ()
        late = (12, 10, 14)
        first = compress_first(me, echoes, replica, [8, 9], width)
        received = {offset: send(piece, offset) for offset, piece in first.items()}
        pieces = compress(me, echoes, sibling, replica, first[8], [12], late, width)
        others = [10, 2, 14, 4, 6, 0]
        pieces.update(compress(me, echoes, sibling, replica, pieces[12][1], others, late, width))
        received.update({offset: send(pieces[offset][0], offset) for offset in [12] + others})
        received_late = {offset: send(pieces[offset][1], offset) for offset in late}
    else:
        late = ()
        pieces = compress(me, echoes, sibling, replica, me, list(range(2, count, 2)) + [0], late, width)
        received = {offset: send(piece, offset) for offset, (piece, _) in pieces.items()}

    forward, inverse = (jnp.asarray(m) for m in phase_matrices(pulses))
    tiles = width // TILE
    spectra, pulse_mask, range_mask, inside = make_tables(
        me, azimuth_replicas, azimuth_extent, range_extent, forward, received[0], width
    )
    tables = (me, forward, inverse, spectra, replica_index[None, :], pulse_mask, range_mask)
    early = [cell for cell in cells if not (chunked and cell in LATE)]
    places = {offset: list(range(len(early))) if offset in late else early for offset in received}
    focused, sums, left, right = focus(
        True, early, places, pulses, width, tiles, tables, received, ()
    )
    from_right = lax.ppermute(left, "row", [(i, i - 1) for i in range(1, count)])
    from_left = lax.ppermute(right, "row", [(i, i + 1) for i in range(count - 1)])
    if not chunked:
        pad = jnp.zeros((tiles - 2, sums.shape[1]), F32)
        edges = jnp.concatenate([from_left, pad, from_right], axis=0)
        return focused.reshape(pulses, 2, width), (sums + edges) / inside
    places = {offset: list(range(len(LATE))) if offset in late else LATE for offset in received}
    sources = {offset: received_late.get(offset, received[offset]) for offset in received}
    more = (focused, sums, from_left, from_right, inside)
    focused, looked = focus(
        False, LATE, places, pulses, width, tiles, tables, sources, more
    )
    return focused.reshape(pulses, 2, width), looked


def solution(mesh):
    return jax.shard_map(
        per_device,
        mesh=mesh,
        in_specs=(
            P(("scene", "row"), None, None),
            P(),
            P(),
            P(("scene", "row")),
            P("scene"),
            P("scene"),
        ),
        out_specs=(P("scene", None, "row"), P(("scene", "row"), None)),
        check_vma=False,
    )
```

```python
import functools

import jax
import jax.numpy as jnp
import ml_dtypes
import numpy as np
from jax import lax
from jax.experimental import pallas as pl
from jax.experimental.pallas import tpu as pltpu
from jax.sharding import PartitionSpec as P

TILE = 16
RADIX = 4
CELL = 128
F32 = jnp.float32
BF16 = jnp.bfloat16
FIRST_VMEM = 24 << 20
RANGE_VMEM = 24 << 20
GATE_VMEM = 1 << 20
FOCUS_VMEM = 24 << 20
SMALL_COST = pl.CostEstimate(flops=1 << 20, bytes_accessed=1 << 16, transcendentals=0)


def dot(a, b):
    return jnp.dot(a, b, preferred_element_type=F32)


def dot_nt(a, b):
    return lax.dot_general(a, b, (((1,), (1,)), ((), ())), preferred_element_type=F32)


def split(x):
    high = x.astype(BF16)
    low = (x - high.astype(F32)).astype(BF16)
    return high, low


def twice(x):
    return jnp.concatenate([x, x], axis=0)


def two_terms(matrix):
    high = matrix.astype(ml_dtypes.bfloat16)
    low = (matrix - high.astype(np.float64)).astype(ml_dtypes.bfloat16)
    return np.concatenate([high, low], axis=2)


@functools.lru_cache(maxsize=None)
def phase_matrices(length):
    part = length // RADIX
    index = np.arange(part)
    k = index.reshape(part // RADIX, RADIX).T.reshape(-1)
    step = np.arange(RADIX)[:, None, None]
    phase = (k[None, :, None] * (RADIX * index[None, None, :] + step)) % length
    angle = phase * (2.0 * np.pi / length)
    cos, sin = np.cos(angle), np.sin(angle)
    forward = two_terms(np.concatenate([cos, -sin], axis=1))
    inverse = two_terms(np.concatenate([cos, sin], axis=2).reshape(RADIX, part, 2, part).transpose(0, 2, 3, 1).reshape(RADIX, 2 * part, part))
    return forward, inverse


def complex_product(matrix, x):
    product = dot(matrix, twice(x))
    rows, lanes = product.shape[0] // 2, product.shape[1] // 2
    real = product[:rows, :lanes] - product[rows:, lanes:]
    imag = product[:rows, lanes:] + product[rows:, :lanes]
    return real, imag


def butterfly(x, sign):
    (ar, ai), (br, bi), (cr, ci), (dr, di) = x
    pr, pi, mr, mi = ar + cr, ai + ci, ar - cr, ai - ci
    sr, si, tr, ti = br + dr, bi + di, br - dr, bi - di
    if sign < 0:
        tr, ti = ti, -tr
    else:
        tr, ti = -ti, tr
    return [(pr + sr, pi + si), (mr + tr, mi + ti), (pr - sr, pi - si), (mr - tr, mi - ti)]


def spectrum_part(values, r):
    rows = values[0][0].shape[0] // RADIX
    span = slice(r * rows, (r + 1) * rows)
    parts = butterfly([(re[span], im[span]) for re, im in values], -1)
    return [jnp.concatenate([p[c] for p in parts], axis=0) for c in range(2)]


def table_kernel(h_ref, table):
    block = table.shape[1]
    for part in range(2):
        lines = jnp.broadcast_to(h_ref[part : part + 1], (block, h_ref.shape[1]))
        table[part] = pltpu.roll(lines, 0, 1, stride=1, stride_axis=0).astype(BF16)


def windows(x_refs, base, width, blocks, count):
    pieces = []
    for step in range(blocks):
        place = base + step
        start = pl.multiple_of(jnp.minimum(place, count - 1) * width, width)
        pieces.append([x_ref.at[:, :, pl.ds(start, width)] for x_ref in x_refs])
    return pieces


def pulse_order(total, swapped):
    row = lax.broadcasted_iota(jnp.int32, (2 * total, 2 * total), 0)
    column = lax.broadcasted_iota(jnp.int32, (2 * total, 2 * total), 1)
    quarter = total // RADIX
    pulse = RADIX * (row % quarter) + (row % total) // quarter
    source = 2 * pulse + row // total
    source = jnp.where(swapped, (source + total) % (2 * total), source)
    return (column == source).astype(F32).astype(BF16)


def correlate(window, table, width, early_out, late_out):
    block = table.shape[1]
    taps = table.shape[2] - block
    total = window.shape[0] // 2
    stacked = jnp.concatenate(
        [window[:, j * block : j * block + block + taps] for j in range(width // block)], axis=0
    )
    with_real = dot_nt(stacked, table[0])
    with_imag = dot_nt(stacked, table[1])
    placed = [0, 0]
    for cell in range(width // CELL):
        at = 2 * total * (cell * CELL // block)
        re, im = slice(at, at + total), slice(at + total, at + 2 * total)
        lanes = slice(cell * CELL % block, cell * CELL % block + CELL)
        real = with_real[re, lanes] + with_imag[im, lanes]
        imag = with_real[im, lanes] - with_imag[re, lanes]
        late = late_out is not None and cell in LATE
        out = late_out if late else early_out
        place = placed[late]
        placed[late] += 1
        out[:, 2 * CELL * place : 2 * CELL * (place + 1)] = jnp.concatenate(
            [real.astype(BF16), imag.astype(BF16)], axis=1
        )


def first_range_kernel(offsets, width, me_ref, x_hbm, h_ref, *refs):
    outs, (table, x_ref, sems) = refs[:-3], refs[-3:]
    rows = x_hbm.shape[0]
    count = x_hbm.shape[2] // width
    blocks = x_ref.shape[0]
    me = me_ref[0]
    base = me ^ offsets[0]
    base = base - base % 2
    copies = []
    for step, (piece,) in enumerate(windows([x_hbm], base, width, blocks, count)):
        copies.append(pltpu.make_async_copy(piece, x_ref.at[step], sems.at[step]))
    for copy in copies:
        copy.start()
    table_kernel(h_ref, table)
    order = pulse_order(rows, False)
    for copy in copies:
        copy.wait()
    pieces = []
    for step in range(blocks):
        piece = x_ref[step].reshape(2 * rows, width)
        pieces.append(jnp.where(base + step < count, piece, jnp.zeros_like(piece)))
    window = dot(order, jnp.concatenate(pieces, axis=1)).astype(BF16)
    reach = window.shape[1] - width
    for offset, out in zip(offsets, outs):
        odd = (me ^ offset) % 2
        mine = jnp.where(odd == 0, window[:, :reach], window[:, width:])
        correlate(mine, table, width, out, None)


def range_kernel(offsets, late, width, me_ref, x_ref, sibling_ref, h_ref, after_ref, *refs):
    del after_ref
    outs, table = refs[:-1], refs[-1]
    table_kernel(h_ref, table)
    rows = x_ref.shape[0]
    taps = table.shape[2] - table.shape[1]
    count = x_ref.shape[2] // width
    me = me_ref[0]
    order = pulse_order(2 * rows, me % 2 == 1)
    outs = iter(outs)
    for offset in offsets:
        owner = me ^ offset
        pieces = []
        for step, piece in enumerate(
            windows([x_ref, sibling_ref], owner, width, 1 + -(-taps // width), count)
        ):
            piece = jnp.concatenate([part[...].reshape(2 * rows, width) for part in piece], axis=0)
            if step:
                piece = jnp.where(owner + step < count, piece, jnp.zeros_like(piece))
            pieces.append(piece)
        window = dot(order, jnp.concatenate(pieces, axis=1)).astype(BF16)
        early_out = next(outs)
        late_out = next(outs) if offset in late else None
        correlate(window, table, width, early_out, late_out)


LATE = (1, 2)


def compress_first(me, echoes, replica, offsets, width):
    rows = echoes.shape[0]
    block = min(256, width)
    taps = replica.shape[1] - block
    blocks = 2 + -(-taps // width)
    vmem = pl.BlockSpec(memory_space=pltpu.VMEM)
    outs = pl.pallas_call(
        functools.partial(first_range_kernel, tuple(offsets), width),
        out_shape=[jax.ShapeDtypeStruct((rows, 2 * width), BF16)] * len(offsets),
        in_specs=[pl.BlockSpec(memory_space=pltpu.SMEM), pl.BlockSpec(memory_space=pl.ANY), vmem],
        out_specs=[vmem] * len(offsets),
        scratch_shapes=[
            pltpu.VMEM((2, block, taps + block), BF16),
            pltpu.VMEM((blocks, rows, 2, width), BF16),
            pltpu.SemaphoreType.DMA((blocks,)),
        ],
        compiler_params=pltpu.CompilerParams(vmem_limit_bytes=FIRST_VMEM),
        cost_estimate=pl.CostEstimate(
            flops=len(offsets) * 16 * rows * width * (taps + 256),
            bytes_accessed=len(offsets) * 4 * rows * width * 3,
            transcendentals=0,
        ),
        name="range_compress_first",
    )(me, echoes, replica)
    return dict(zip(offsets, outs))


def compress(me, echoes, sibling, replica, after, offsets, late, width):
    total = 2 * echoes.shape[0]
    block = min(256, width)
    taps = replica.shape[1] - block
    vmem = pl.BlockSpec(memory_space=pltpu.VMEM)
    shapes = []
    for offset in offsets:
        if offset in late:
            shapes += [(total, 2 * (width - len(LATE) * CELL)), (total, 2 * len(LATE) * CELL)]
        else:
            shapes += [(total, 2 * width)]
    outs = pl.pallas_call(
        functools.partial(range_kernel, tuple(offsets), late, width),
        out_shape=[jax.ShapeDtypeStruct(shape, BF16) for shape in shapes],
        in_specs=[pl.BlockSpec(memory_space=pltpu.SMEM), vmem, vmem, vmem, pl.BlockSpec(memory_space=pl.ANY)],
        out_specs=[vmem] * len(shapes),
        scratch_shapes=[pltpu.VMEM((2, block, taps + block), BF16)],
        compiler_params=pltpu.CompilerParams(vmem_limit_bytes=RANGE_VMEM),
        cost_estimate=pl.CostEstimate(
            flops=len(offsets) * 16 * total * width * (taps + block),
            bytes_accessed=len(offsets) * 4 * total * width * 3,
            transcendentals=0,
        ),
        name="range_compress",
    )(me, echoes, sibling, replica, after)
    outs = iter(outs)
    return {offset: (next(outs), next(outs) if offset in late else None) for offset in offsets}


def gate_kernel(*refs):
    del refs


def gate(pieces, after):
    anywhere = pl.BlockSpec(memory_space=pl.ANY)
    return pl.pallas_call(
        gate_kernel,
        out_shape=[jax.ShapeDtypeStruct(piece.shape, piece.dtype) for piece in pieces],
        in_specs=[anywhere] * (len(pieces) + len(after)),
        out_specs=[anywhere] * len(pieces),
        input_output_aliases={n: n for n in range(len(pieces))},
        compiler_params=pltpu.CompilerParams(vmem_limit_bytes=GATE_VMEM),
        cost_estimate=SMALL_COST,
        name="gate",
    )(*pieces, *after)


def column(line, select):
    return jnp.sum(jnp.where(select, line, 0.0), axis=1, keepdims=True)


def tables_kernel(
    me_ref, taps_ref, azimuth_ref, range_ref, matrix_ref, after_ref,
    spectra_ref, pulse_ref, mask_ref, inside_ref,
):
    del after_ref
    part = matrix_ref.shape[1] // 2
    length = part * RADIX
    replicas, _, tap_count = taps_ref.shape
    row = lax.broadcasted_iota(jnp.int32, (2 * CELL, 2 * replicas), 0)
    source = lax.broadcasted_iota(jnp.int32, (2 * CELL, 2 * replicas), 1)
    place = (row % CELL < replicas) & (source == 2 * (row % CELL) + row // CELL)
    taps = taps_ref[...].reshape(2 * replicas, tap_count)
    taps = dot(place.astype(F32).astype(BF16), taps).astype(BF16)
    m = lax.broadcasted_iota(jnp.int32, (part, tap_count), 0)
    tap = lax.broadcasted_iota(jnp.int32, (part, tap_count), 1)
    values = []
    for q in range(RADIX):
        pick = (tap == RADIX * m + q).astype(F32).astype(BF16)
        values.append(complex_product(matrix_ref[q], dot_nt(pick, taps).astype(BF16)))
    for r in range(RADIX):
        spectrum = jnp.concatenate(spectrum_part(values, r), axis=0) * (1.0 / length)
        high, low = split(spectrum)
        spectra_ref[r] = jnp.concatenate([high[:, :replicas], low[:, :replicas]], axis=1)

    def mask(starts, stops, at):
        at = at.astype(F32)
        return ((at >= starts) & (at < stops)).astype(F32).astype(BF16)

    pulse_tiles = azimuth_ref.shape[1]
    extents = azimuth_ref[...].astype(F32)
    row = lax.broadcasted_iota(jnp.int32, (pulse_tiles, pulse_tiles), 0)
    lane = lax.broadcasted_iota(jnp.int32, (pulse_tiles, pulse_tiles), 1)
    extent = column(extents, row == lane)
    start = (TILE * lax.broadcasted_iota(jnp.int32, (pulse_tiles, 1), 0)).astype(F32)
    lane = lax.broadcasted_iota(jnp.int32, pulse_ref.shape, 1)
    pulse_ref[...] = mask(start - extent, start + TILE + extent, RADIX * (lane % part) + lane // part)
    start = (TILE * lax.broadcasted_iota(jnp.int32, (1, pulse_tiles), 1)).astype(F32)
    pulse_count = jnp.minimum(start + TILE + extents, 1.0 * length) - jnp.maximum(start - extents, 0.0)

    tiles = inside_ref.shape[0]
    mask_rows, width = mask_ref.shape
    total = range_ref.shape[1]
    row = lax.broadcasted_iota(jnp.int32, (mask_rows, 1), 0)
    tile = me_ref[0] * tiles + jnp.where(row == tiles, -1, jnp.where(row == tiles + 1, tiles, row))
    exists = (row < tiles + 2) & (tile >= 0) & (tile < total)
    lane = lax.broadcasted_iota(jnp.int32, (mask_rows, total), 1)
    extent = column(range_ref[...].astype(F32), lane == tile)
    start = (TILE * tile).astype(F32) - extent
    stop = (TILE * tile + TILE).astype(F32) + extent
    lane = lax.broadcasted_iota(jnp.int32, mask_ref.shape, 1)
    mask_ref[...] = mask(start, jnp.where(exists, stop, start), me_ref[0] * width + lane)
    count = jnp.minimum(stop, 1.0 * TILE * total) - jnp.maximum(start, 0.0)
    inside_ref[...] = count[:tiles] * pulse_count


def make_tables(me, azimuth_replicas, azimuth_extent, range_extent, matrix, after, width):
    part = matrix.shape[1] // 2
    replicas = azimuth_replicas.shape[0]
    pulse_tiles = azimuth_extent.shape[0]
    tiles = width // TILE
    mask_rows = -(-(tiles + 2) // 16) * 16
    vmem = pl.BlockSpec(memory_space=pltpu.VMEM)
    shapes = [
        ((RADIX, 2 * part, 2 * replicas), BF16),
        ((pulse_tiles, RADIX * part), BF16),
        ((mask_rows, width), BF16),
        ((tiles, pulse_tiles), F32),
    ]
    return pl.pallas_call(
        tables_kernel,
        out_shape=[jax.ShapeDtypeStruct(*shape) for shape in shapes],
        in_specs=[pl.BlockSpec(memory_space=pltpu.SMEM)] + [vmem] * 4 + [pl.BlockSpec(memory_space=pl.ANY)],
        out_specs=[vmem] * 4,
        compiler_params=pltpu.CompilerParams(vmem_limit_bytes=RANGE_VMEM),
        cost_estimate=pl.CostEstimate(flops=1 << 31, bytes_accessed=4 << 20, transcendentals=0),
        name="tables",
    )(me, azimuth_replicas, azimuth_extent[None, :], range_extent[None, :], matrix, after)


def gather_pulses(offsets, places, n, sources, me, total, x_ref):
    direct = x_ref.shape[0] == RADIX
    for offset, source in zip(offsets, sources):
        at = slice(2 * CELL * places[offset][n], 2 * CELL * (places[offset][n] + 1))
        rows = source.shape[0]
        owner = (me ^ offset) // (2 * rows // total)
        rows = rows // RADIX if direct else rows
        start = pl.multiple_of(owner * rows, rows)
        if direct:
            for q in range(RADIX):
                span = slice(q * rows, (q + 1) * rows)
                x_ref[q, pl.ds(start, rows), :] = source[span, at]
        else:
            x_ref[pl.ds(start, rows), :] = source[:, at]


def pulses_of(x_ref, q, total, part):
    if x_ref.shape[0] == RADIX:
        return x_ref[q]
    quarter = total // RADIX
    m = lax.broadcasted_iota(jnp.int32, (part, x_ref.shape[0]), 0)
    row = lax.broadcasted_iota(jnp.int32, (part, x_ref.shape[0]), 1)
    pick = row == (m // quarter) * total + q * quarter + m % quarter
    return dot(pick.astype(F32).astype(BF16), x_ref[...]).astype(BF16)


def focus_kernel(
    offsets, places, cells, first, me_ref, forward_ref, inverse_ref, spectra_ref, index_ref, pulse_ref, range_ref, *refs
):
    sources, refs = refs[: len(offsets)], refs[len(offsets) :]
    if first:
        focused_hbm, sums_ref, left_ref, right_ref = refs[:4]
        tiles = sums_ref.shape[0]
    else:
        _, focused_hbm, sums_ref = refs[:3]
        tiles = sums_ref.shape[0]
    x_ref, v_ref, s_ref, power_ref, image_ref, sems = refs[-6:]
    total = max(source.shape[0] for source in sources)
    part = v_ref.shape[3]
    me = me_ref[0]
    steps = range(len(cells))
    for n in steps:
        gather_pulses(offsets, places, n, sources, me, total, x_ref.at[n])
    replicas = spectra_ref.shape[2] // 2
    row = lax.broadcasted_iota(jnp.int32, (2 * replicas, CELL), 0)

    def transform(n):
        for q in range(RADIX):
            x = pulses_of(x_ref.at[n], q, total, part)
            v_ref[n, q, 0], v_ref[n, q, 1] = complex_product(forward_ref[q], x)

    def correlate_cell(n):
        lanes = slice(cells[n] * CELL, (cells[n] + 1) * CELL)
        chosen = (row % replicas == index_ref[:, lanes]).astype(F32).astype(BF16)
        rows = part // RADIX
        for r in range(RADIX):
            span = slice(r * rows, (r + 1) * rows)
            x = butterfly([(v_ref[n, q, 0, span], v_ref[n, q, 1, span]) for q in range(RADIX)], -1)
            replica = dot(spectra_ref[r], chosen)
            y = []
            for j, (sr, si) in enumerate(x):
                gr = replica[j * rows : (j + 1) * rows]
                gi = replica[part + j * rows : part + (j + 1) * rows]
                y.append((sr * gr + si * gi, si * gr - sr * gi))
            for q, (re, im) in enumerate(butterfly(y, 1)):
                s_ref[n, q, span, :CELL] = re.astype(BF16)
                s_ref[n, q, span, CELL:] = im.astype(BF16)

    copies = []

    def finish(n):
        lanes = slice(cells[n] * CELL, (cells[n] + 1) * CELL)
        for q in range(RADIX):
            re, im = complex_product(inverse_ref[q], s_ref[n, q])
            both = jnp.stack([re.astype(BF16), im.astype(BF16)], axis=0)
            image_ref[n, q] = jnp.swapaxes(both, 0, 1)
            copy = pltpu.make_async_copy(
                image_ref.at[n, q], focused_hbm.at[:, q, :, lanes], sems.at[n, q]
            )
            copy.start()
            copies.append(copy)
            power = (re * re + im * im).astype(BF16)
            power_ref[q * part : (q + 1) * part, n * CELL : (n + 1) * CELL] = power

    for n in steps:
        transform(n)
    for n in steps:
        correlate_cell(n)
    for n in steps:
        finish(n)
    sums = dot(pulse_ref[...], power_ref[...])
    high, low = split(sums)
    mask = jnp.concatenate([range_ref[:, cell * CELL : (cell + 1) * CELL] for cell in cells], axis=1)
    sums = dot_nt(jnp.concatenate([mask, mask], axis=1), jnp.concatenate([high, low], axis=1))
    sums_ref[...] = sums[:tiles]
    if first:
        left_ref[...] = sums[tiles : tiles + 1]
        right_ref[...] = sums[tiles + 1 : tiles + 2]
    for copy in copies:
        copy.wait()


def focus(first, cells, places, pulses, width, tiles, tables, sources, more):
    me, forward, inverse, spectra, index, pulse_mask, range_mask = tables
    pulse_tiles = pulse_mask.shape[0]
    part = pulses // RADIX
    offsets = list(sources)
    vmem = pl.BlockSpec(memory_space=pltpu.VMEM)
    anywhere = pl.BlockSpec(memory_space=pl.ANY)
    in_specs = [pl.BlockSpec(memory_space=pltpu.SMEM)] + [vmem] * (6 + len(offsets))
    shapes = [jax.ShapeDtypeStruct((part, RADIX, 2, width), BF16)]
    shapes += [jax.ShapeDtypeStruct((tiles, pulse_tiles), F32)]
    if first:
        shapes += [jax.ShapeDtypeStruct((1, pulse_tiles), F32)] * 2
    else:
        in_specs += [anywhere]
    direct = all(source.shape[0] % (16 * RADIX) == 0 for source in sources.values())
    x_shape = (RADIX, part, 2 * CELL) if direct else (pulses, 2 * CELL)
    return pl.pallas_call(
        functools.partial(focus_kernel, tuple(offsets), places, tuple(cells), first),
        out_shape=shapes,
        in_specs=in_specs,
        out_specs=[anywhere] + [vmem] * (len(shapes) - 1),
        scratch_shapes=[
            pltpu.VMEM((len(cells),) + x_shape, BF16),
            pltpu.VMEM((len(cells), RADIX, 2, part, CELL), F32),
            pltpu.VMEM((len(cells), RADIX, part, 2 * CELL), BF16),
            pltpu.VMEM((pulses, len(cells) * CELL), BF16),
            pltpu.VMEM((len(cells), RADIX, part, 2, CELL), BF16),
            pltpu.SemaphoreType.DMA((len(cells), RADIX)),
        ],
        input_output_aliases={} if first else {7 + len(offsets): 0},
        compiler_params=pltpu.CompilerParams(vmem_limit_bytes=FOCUS_VMEM),
        cost_estimate=pl.CostEstimate(
            flops=len(cells) << 31, bytes_accessed=len(cells) << 21, transcendentals=0
        ),
        name="azimuth_focus",
    )(me, forward, inverse, spectra, index, pulse_mask, range_mask, *sources.values(), *more)


def looks_kernel(from_left_ref, from_right_ref, inside_ref, *refs):
    sums = sum(ref[...] for ref in refs[:-1])
    row = lax.broadcasted_iota(jnp.int32, sums.shape, 0)
    sums += jnp.where(row == 0, from_left_ref[...], 0.0)
    sums += jnp.where(row == sums.shape[0] - 1, from_right_ref[...], 0.0)
    refs[-1][...] = sums / inside_ref[...]


def looks(from_left, from_right, inside, *sums):
    return pl.pallas_call(
        looks_kernel,
        out_shape=jax.ShapeDtypeStruct(inside.shape, F32),
        compiler_params=pltpu.CompilerParams(vmem_limit_bytes=GATE_VMEM),
        cost_estimate=SMALL_COST,
        name="looks",
    )(from_left, from_right, inside, *sums)


def per_device(
    echoes, range_replica, azimuth_replicas, replica_index, azimuth_extent, range_extent
):
    count = lax.axis_size("row")
    device = lax.axis_index("row")
    me = device.astype(jnp.int32)[None]
    rows, _, samples = echoes.shape
    pulses = rows * count
    width = samples // count
    cells = list(range(width // CELL))
    chunked = len(cells) == RADIX and count == 16

    def send(piece, offset):
        if offset == 0:
            return piece
        return lax.ppermute(piece, "row", [(i, i ^ offset) for i in range(count)])

    sibling = send(echoes, 1)
    replica = jnp.pad(range_replica.astype(F32), ((0, 0), (0, min(256, width))))
    if chunked:
        late = ()
        late = (12, 10, 14)
        first = compress_first(me, echoes, replica, [8, 9], width)
        received = {offset: send(piece, offset) for offset, piece in first.items()}
        pieces = compress(me, echoes, sibling, replica, first[8], [12], late, width)
        others = [10, 2, 14, 4, 6, 0]
        pieces.update(compress(me, echoes, sibling, replica, pieces[12][1], others, late, width))
        received.update({offset: send(pieces[offset][0], offset) for offset in [12] + others})
        received_late = {offset: send(pieces[offset][1], offset) for offset in late}
    else:
        late = ()
        pieces = compress(me, echoes, sibling, replica, me, list(range(2, count, 2)) + [0], late, width)
        received = {offset: send(piece, offset) for offset, (piece, _) in pieces.items()}

    forward, inverse = (jnp.asarray(m) for m in phase_matrices(pulses))
    tiles = width // TILE
    spectra, pulse_mask, range_mask, inside = make_tables(
        me, azimuth_replicas, azimuth_extent, range_extent, forward, received[0], width
    )
    tables = (me, forward, inverse, spectra, replica_index[None, :], pulse_mask, range_mask)
    early = [cell for cell in cells if not (chunked and cell in LATE)]
    places = {offset: list(range(len(early))) if offset in late else early for offset in received}
    focused, sums, left, right = focus(
        True, early, places, pulses, width, tiles, tables, received, ()
    )
    from_right = lax.ppermute(left, "row", [(i, i - 1) for i in range(1, count)])
    from_left = lax.ppermute(right, "row", [(i, i + 1) for i in range(count - 1)])
    sums = [sums]
    if chunked:
        places = {offset: list(range(len(LATE))) if offset in late else LATE for offset in received}
        sources = {offset: received_late.get(offset, received[offset]) for offset in received}
        focused, late_sums = focus(
            False, LATE, places, pulses, width, tiles, tables, sources, (focused,)
        )
        sums.append(late_sums)
    return focused.reshape(pulses, 2, width), looks(from_left, from_right, inside, *sums)


def solution(mesh):
    return jax.shard_map(
        per_device,
        mesh=mesh,
        in_specs=(
            P(("scene", "row"), None, None),
            P(),
            P(),
            P(("scene", "row")),
            P("scene"),
            P("scene"),
        ),
        out_specs=(P("scene", None, "row"), P(("scene", "row"), None)),
        check_vma=False,
    )
```

```python
import functools

import jax
import jax.numpy as jnp
import ml_dtypes
import numpy as np
from jax import lax
from jax.experimental import pallas as pl
from jax.experimental.pallas import tpu as pltpu
from jax.sharding import PartitionSpec as P

TILE = 16
RADIX = 4
CELL = 128
F32 = jnp.float32
BF16 = jnp.bfloat16
FIRST_VMEM = 24 << 20
RANGE_VMEM = 24 << 20
GATE_VMEM = 1 << 20
FOCUS_VMEM = 24 << 20
SMALL_COST = pl.CostEstimate(flops=1 << 20, bytes_accessed=1 << 16, transcendentals=0)


def dot(a, b):
    return jnp.dot(a, b, preferred_element_type=F32)


def dot_nt(a, b):
    return lax.dot_general(a, b, (((1,), (1,)), ((), ())), preferred_element_type=F32)


def split(x):
    high = x.astype(BF16)
    low = (x - high.astype(F32)).astype(BF16)
    return high, low


def twice(x):
    return jnp.concatenate([x, x], axis=0)


def two_terms(matrix):
    high = matrix.astype(ml_dtypes.bfloat16)
    low = (matrix - high.astype(np.float64)).astype(ml_dtypes.bfloat16)
    return np.concatenate([high, low], axis=2)


@functools.lru_cache(maxsize=None)
def phase_matrices(length):
    part = length // RADIX
    index = np.arange(part)
    k = index.reshape(part // RADIX, RADIX).T.reshape(-1)
    step = np.arange(RADIX)[:, None, None]
    phase = (k[None, :, None] * (RADIX * index[None, None, :] + step)) % length
    angle = phase * (2.0 * np.pi / length)
    cos, sin = np.cos(angle), np.sin(angle)
    forward = two_terms(np.concatenate([cos, -sin], axis=1))
    inverse = two_terms(np.concatenate([cos, sin], axis=2).reshape(RADIX, part, 2, part).transpose(0, 2, 3, 1).reshape(RADIX, 2 * part, part))
    return forward, inverse


def complex_product(matrix, x):
    product = dot(matrix, twice(x))
    rows, lanes = product.shape[0] // 2, product.shape[1] // 2
    real = product[:rows, :lanes] - product[rows:, lanes:]
    imag = product[:rows, lanes:] + product[rows:, :lanes]
    return real, imag


def butterfly(x, sign):
    (ar, ai), (br, bi), (cr, ci), (dr, di) = x
    pr, pi, mr, mi = ar + cr, ai + ci, ar - cr, ai - ci
    sr, si, tr, ti = br + dr, bi + di, br - dr, bi - di
    if sign < 0:
        tr, ti = ti, -tr
    else:
        tr, ti = -ti, tr
    return [(pr + sr, pi + si), (mr + tr, mi + ti), (pr - sr, pi - si), (mr - tr, mi - ti)]


def spectrum_part(values, r):
    rows = values[0][0].shape[0] // RADIX
    span = slice(r * rows, (r + 1) * rows)
    parts = butterfly([(re[span], im[span]) for re, im in values], -1)
    return [jnp.concatenate([p[c] for p in parts], axis=0) for c in range(2)]


def table_kernel(h_ref, table):
    block = table.shape[1]
    for part in range(2):
        lines = jnp.broadcast_to(h_ref[part : part + 1], (block, h_ref.shape[1]))
        table[part] = pltpu.roll(lines, 0, 1, stride=1, stride_axis=0).astype(BF16)


def windows(x_refs, base, width, blocks, count):
    pieces = []
    for step in range(blocks):
        place = base + step
        start = pl.multiple_of(jnp.minimum(place, count - 1) * width, width)
        pieces.append([x_ref.at[:, :, pl.ds(start, width)] for x_ref in x_refs])
    return pieces


def pulse_order(total, swapped):
    row = lax.broadcasted_iota(jnp.int32, (2 * total, 2 * total), 0)
    column = lax.broadcasted_iota(jnp.int32, (2 * total, 2 * total), 1)
    quarter = total // RADIX
    pulse = RADIX * (row % quarter) + (row % total) // quarter
    source = 2 * pulse + row // total
    source = jnp.where(swapped, (source + total) % (2 * total), source)
    return (column == source).astype(F32).astype(BF16)


def correlate(window, table, width, early_out, late_out):
    block = table.shape[1]
    taps = table.shape[2] - block
    total = window.shape[0] // 2
    stacked = jnp.concatenate(
        [window[:, j * block : j * block + block + taps] for j in range(width // block)], axis=0
    )
    with_real = dot_nt(stacked, table[0])
    with_imag = dot_nt(stacked, table[1])
    placed = [0, 0]
    for cell in range(width // CELL):
        at = 2 * total * (cell * CELL // block)
        re, im = slice(at, at + total), slice(at + total, at + 2 * total)
        lanes = slice(cell * CELL % block, cell * CELL % block + CELL)
        real = with_real[re, lanes] + with_imag[im, lanes]
        imag = with_real[im, lanes] - with_imag[re, lanes]
        late = late_out is not None and cell in LATE
        out = late_out if late else early_out
        place = placed[late]
        placed[late] += 1
        out[:, 2 * CELL * place : 2 * CELL * (place + 1)] = jnp.concatenate(
            [real.astype(BF16), imag.astype(BF16)], axis=1
        )


def first_range_kernel(offsets, width, me_ref, x_hbm, h_ref, *refs):
    outs, (table, x_ref, sems) = refs[:-3], refs[-3:]
    rows = x_hbm.shape[0]
    count = x_hbm.shape[2] // width
    blocks = x_ref.shape[0]
    me = me_ref[0]
    base = me ^ offsets[0]
    base = base - base % 2
    copies = []
    for step, (piece,) in enumerate(windows([x_hbm], base, width, blocks, count)):
        copies.append(pltpu.make_async_copy(piece, x_ref.at[step], sems.at[step]))
    for copy in copies:
        copy.start()
    table_kernel(h_ref, table)
    order = pulse_order(rows, False)
    for copy in copies:
        copy.wait()
    pieces = []
    for step in range(blocks):
        piece = x_ref[step].reshape(2 * rows, width)
        pieces.append(jnp.where(base + step < count, piece, jnp.zeros_like(piece)))
    window = dot(order, jnp.concatenate(pieces, axis=1)).astype(BF16)
    reach = window.shape[1] - width
    for offset, out in zip(offsets, outs):
        odd = (me ^ offset) % 2
        mine = jnp.where(odd == 0, window[:, :reach], window[:, width:])
        correlate(mine, table, width, out, None)


def range_kernel(offsets, late, width, me_ref, x_ref, sibling_ref, h_ref, after_ref, *refs):
    del after_ref
    outs, table = refs[:-1], refs[-1]
    table_kernel(h_ref, table)
    rows = x_ref.shape[0]
    taps = table.shape[2] - table.shape[1]
    count = x_ref.shape[2] // width
    me = me_ref[0]
    order = pulse_order(2 * rows, me % 2 == 1)
    outs = iter(outs)
    for offset in offsets:
        owner = me ^ offset
        pieces = []
        for step, piece in enumerate(
            windows([x_ref, sibling_ref], owner, width, 1 + -(-taps // width), count)
        ):
            piece = jnp.concatenate([part[...].reshape(2 * rows, width) for part in piece], axis=0)
            if step:
                piece = jnp.where(owner + step < count, piece, jnp.zeros_like(piece))
            pieces.append(piece)
        window = dot(order, jnp.concatenate(pieces, axis=1)).astype(BF16)
        early_out = next(outs)
        late_out = next(outs) if offset in late else None
        correlate(window, table, width, early_out, late_out)


LATE = (1, 2)


def compress_first(me, echoes, replica, offsets, width):
    rows = echoes.shape[0]
    block = min(256, width)
    taps = replica.shape[1] - block
    blocks = 2 + -(-taps // width)
    vmem = pl.BlockSpec(memory_space=pltpu.VMEM)
    outs = pl.pallas_call(
        functools.partial(first_range_kernel, tuple(offsets), width),
        out_shape=[jax.ShapeDtypeStruct((rows, 2 * width), BF16)] * len(offsets),
        in_specs=[pl.BlockSpec(memory_space=pltpu.SMEM), pl.BlockSpec(memory_space=pl.ANY), vmem],
        out_specs=[vmem] * len(offsets),
        scratch_shapes=[
            pltpu.VMEM((2, block, taps + block), BF16),
            pltpu.VMEM((blocks, rows, 2, width), BF16),
            pltpu.SemaphoreType.DMA((blocks,)),
        ],
        compiler_params=pltpu.CompilerParams(vmem_limit_bytes=FIRST_VMEM),
        cost_estimate=pl.CostEstimate(
            flops=len(offsets) * 16 * rows * width * (taps + 256),
            bytes_accessed=len(offsets) * 4 * rows * width * 3,
            transcendentals=0,
        ),
        name="range_compress_first",
    )(me, echoes, replica)
    return dict(zip(offsets, outs))


def compress(me, echoes, sibling, replica, after, offsets, late, width):
    total = 2 * echoes.shape[0]
    block = min(256, width)
    taps = replica.shape[1] - block
    vmem = pl.BlockSpec(memory_space=pltpu.VMEM)
    shapes = []
    for offset in offsets:
        if offset in late:
            shapes += [(total, 2 * (width - len(LATE) * CELL)), (total, 2 * len(LATE) * CELL)]
        else:
            shapes += [(total, 2 * width)]
    outs = pl.pallas_call(
        functools.partial(range_kernel, tuple(offsets), late, width),
        out_shape=[jax.ShapeDtypeStruct(shape, BF16) for shape in shapes],
        in_specs=[pl.BlockSpec(memory_space=pltpu.SMEM), vmem, vmem, vmem, pl.BlockSpec(memory_space=pl.ANY)],
        out_specs=[vmem] * len(shapes),
        scratch_shapes=[pltpu.VMEM((2, block, taps + block), BF16)],
        compiler_params=pltpu.CompilerParams(vmem_limit_bytes=RANGE_VMEM),
        cost_estimate=pl.CostEstimate(
            flops=len(offsets) * 16 * total * width * (taps + block),
            bytes_accessed=len(offsets) * 4 * total * width * 3,
            transcendentals=0,
        ),
        name="range_compress",
    )(me, echoes, sibling, replica, after)
    outs = iter(outs)
    return {offset: (next(outs), next(outs) if offset in late else None) for offset in offsets}


def gate_kernel(*refs):
    del refs


def gate(pieces, after):
    anywhere = pl.BlockSpec(memory_space=pl.ANY)
    return pl.pallas_call(
        gate_kernel,
        out_shape=[jax.ShapeDtypeStruct(piece.shape, piece.dtype) for piece in pieces],
        in_specs=[anywhere] * (len(pieces) + len(after)),
        out_specs=[anywhere] * len(pieces),
        input_output_aliases={n: n for n in range(len(pieces))},
        compiler_params=pltpu.CompilerParams(vmem_limit_bytes=GATE_VMEM),
        cost_estimate=SMALL_COST,
        name="gate",
    )(*pieces, *after)


def column(line, select):
    return jnp.sum(jnp.where(select, line, 0.0), axis=1, keepdims=True)


def tables_kernel(
    me_ref, taps_ref, index_ref, azimuth_ref, range_ref, matrix_ref, after_ref,
    spectra_ref, pulse_ref, mask_ref, inside_ref,
):
    del after_ref
    part = matrix_ref.shape[1] // 2
    length = part * RADIX
    replicas, _, tap_count = taps_ref.shape
    row = lax.broadcasted_iota(jnp.int32, (2 * CELL, 2 * replicas), 0)
    source = lax.broadcasted_iota(jnp.int32, (2 * CELL, 2 * replicas), 1)
    place = (row % CELL < replicas) & (source == 2 * (row % CELL) + row // CELL)
    taps = taps_ref[...].reshape(2 * replicas, tap_count)
    taps = dot(place.astype(F32).astype(BF16), taps).astype(BF16)
    m = lax.broadcasted_iota(jnp.int32, (part, tap_count), 0)
    tap = lax.broadcasted_iota(jnp.int32, (part, tap_count), 1)
    bins = index_ref.shape[1]
    row = lax.broadcasted_iota(jnp.int32, (2 * replicas, bins), 0)
    chosen = (row % replicas == index_ref[...]).astype(F32).astype(BF16)
    values = []
    for q in range(RADIX):
        pick = (tap == RADIX * m + q).astype(F32).astype(BF16)
        values.append(complex_product(matrix_ref[q], dot_nt(pick, taps).astype(BF16)))
    for r in range(RADIX):
        spectrum = jnp.concatenate(spectrum_part(values, r), axis=0) * (1.0 / length)
        high, low = split(spectrum)
        both = jnp.concatenate([high[:, :replicas], low[:, :replicas]], axis=1)
        spectra_ref[r] = dot(both, chosen)

    def mask(starts, stops, at):
        at = at.astype(F32)
        return ((at >= starts) & (at < stops)).astype(F32).astype(BF16)

    pulse_tiles = azimuth_ref.shape[1]
    extents = azimuth_ref[...].astype(F32)
    row = lax.broadcasted_iota(jnp.int32, (pulse_tiles, pulse_tiles), 0)
    lane = lax.broadcasted_iota(jnp.int32, (pulse_tiles, pulse_tiles), 1)
    extent = column(extents, row == lane)
    start = (TILE * lax.broadcasted_iota(jnp.int32, (pulse_tiles, 1), 0)).astype(F32)
    lane = lax.broadcasted_iota(jnp.int32, pulse_ref.shape, 1)
    pulse_ref[...] = mask(start - extent, start + TILE + extent, RADIX * (lane % part) + lane // part)
    start = (TILE * lax.broadcasted_iota(jnp.int32, (1, pulse_tiles), 1)).astype(F32)
    pulse_count = jnp.minimum(start + TILE + extents, 1.0 * length) - jnp.maximum(start - extents, 0.0)

    tiles = inside_ref.shape[0]
    mask_rows, width = mask_ref.shape
    total = range_ref.shape[1]
    row = lax.broadcasted_iota(jnp.int32, (mask_rows, 1), 0)
    tile = me_ref[0] * tiles + jnp.where(row == tiles, -1, jnp.where(row == tiles + 1, tiles, row))
    exists = (row < tiles + 2) & (tile >= 0) & (tile < total)
    lane = lax.broadcasted_iota(jnp.int32, (mask_rows, total), 1)
    extent = column(range_ref[...].astype(F32), lane == tile)
    start = (TILE * tile).astype(F32) - extent
    stop = (TILE * tile + TILE).astype(F32) + extent
    lane = lax.broadcasted_iota(jnp.int32, mask_ref.shape, 1)
    mask_ref[...] = mask(start, jnp.where(exists, stop, start), me_ref[0] * width + lane)
    count = jnp.minimum(stop, 1.0 * TILE * total) - jnp.maximum(start, 0.0)
    inside_ref[...] = count[:tiles] * pulse_count


def make_tables(me, azimuth_replicas, index, azimuth_extent, range_extent, matrix, after, width):
    part = matrix.shape[1] // 2
    replicas = azimuth_replicas.shape[0]
    pulse_tiles = azimuth_extent.shape[0]
    tiles = width // TILE
    mask_rows = -(-(tiles + 2) // 16) * 16
    vmem = pl.BlockSpec(memory_space=pltpu.VMEM)
    shapes = [
        ((RADIX, 2 * part, width), F32),
        ((pulse_tiles, RADIX * part), BF16),
        ((mask_rows, width), BF16),
        ((tiles, pulse_tiles), F32),
    ]
    return pl.pallas_call(
        tables_kernel,
        out_shape=[jax.ShapeDtypeStruct(*shape) for shape in shapes],
        in_specs=[pl.BlockSpec(memory_space=pltpu.SMEM)] + [vmem] * 5 + [pl.BlockSpec(memory_space=pl.ANY)],
        out_specs=[vmem] * 4,
        compiler_params=pltpu.CompilerParams(vmem_limit_bytes=RANGE_VMEM),
        cost_estimate=pl.CostEstimate(flops=1 << 31, bytes_accessed=4 << 20, transcendentals=0),
        name="tables",
    )(me, azimuth_replicas, index, azimuth_extent[None, :], range_extent[None, :], matrix, after)


def gather_pulses(offsets, places, n, sources, me, total, x_ref):
    direct = x_ref.shape[0] == RADIX
    for offset, source in zip(offsets, sources):
        at = slice(2 * CELL * places[offset][n], 2 * CELL * (places[offset][n] + 1))
        rows = source.shape[0]
        owner = (me ^ offset) // (2 * rows // total)
        rows = rows // RADIX if direct else rows
        start = pl.multiple_of(owner * rows, rows)
        if direct:
            for q in range(RADIX):
                span = slice(q * rows, (q + 1) * rows)
                x_ref[q, pl.ds(start, rows), :] = source[span, at]
        else:
            x_ref[pl.ds(start, rows), :] = source[:, at]


def pulses_of(x_ref, q, total, part):
    if x_ref.shape[0] == RADIX:
        return x_ref[q]
    quarter = total // RADIX
    m = lax.broadcasted_iota(jnp.int32, (part, x_ref.shape[0]), 0)
    row = lax.broadcasted_iota(jnp.int32, (part, x_ref.shape[0]), 1)
    pick = row == (m // quarter) * total + q * quarter + m % quarter
    return dot(pick.astype(F32).astype(BF16), x_ref[...]).astype(BF16)


def focus_kernel(
    offsets, places, cells, first, me_ref, forward_ref, inverse_ref, spectra_ref, pulse_ref, range_ref, *refs
):
    sources, refs = refs[: len(offsets)], refs[len(offsets) :]
    if first:
        focused_hbm, sums_ref, left_ref, right_ref = refs[:4]
        tiles = sums_ref.shape[0]
    else:
        _, focused_hbm, sums_ref = refs[:3]
        tiles = sums_ref.shape[0]
    x_ref, v_ref, s_ref, power_ref, image_ref, sems = refs[-6:]
    total = max(source.shape[0] for source in sources)
    part = v_ref.shape[3]
    me = me_ref[0]
    steps = range(len(cells))
    for n in steps:
        gather_pulses(offsets, places, n, sources, me, total, x_ref.at[n])

    def transform(n):
        for q in range(RADIX):
            x = pulses_of(x_ref.at[n], q, total, part)
            v_ref[n, q, 0], v_ref[n, q, 1] = complex_product(forward_ref[q], x)

    def correlate_cell(n):
        lanes = slice(cells[n] * CELL, (cells[n] + 1) * CELL)
        rows = part // RADIX
        for r in range(RADIX):
            span = slice(r * rows, (r + 1) * rows)
            x = butterfly([(v_ref[n, q, 0, span], v_ref[n, q, 1, span]) for q in range(RADIX)], -1)
            y = []
            for j, (sr, si) in enumerate(x):
                gr = spectra_ref[r, j * rows : (j + 1) * rows, lanes]
                gi = spectra_ref[r, part + j * rows : part + (j + 1) * rows, lanes]
                y.append((sr * gr + si * gi, si * gr - sr * gi))
            for q, (re, im) in enumerate(butterfly(y, 1)):
                s_ref[n, q, span, :CELL] = re.astype(BF16)
                s_ref[n, q, span, CELL:] = im.astype(BF16)

    copies = []

    def finish(n):
        lanes = slice(n * CELL, (n + 1) * CELL)
        for q in range(RADIX):
            re, im = complex_product(inverse_ref[q], s_ref[n, q])
            both = jnp.stack([re.astype(BF16), im.astype(BF16)], axis=0)
            image_ref[q, :, :, lanes] = jnp.swapaxes(both, 0, 1)
            power_ref[q * part : (q + 1) * part, lanes] = (re * re + im * im).astype(BF16)
            copy = pltpu.make_async_copy(
                image_ref.at[q, :, :, lanes],
                focused_hbm.at[:, q, :, cells[n] * CELL : (cells[n] + 1) * CELL],
                sems.at[n, q],
            )
            copy.start()
            copies.append(copy)

    for n in steps:
        transform(n)
    for n in steps:
        correlate_cell(n)
        finish(n)
    sums = dot(pulse_ref[...], power_ref[...])
    high, low = split(sums)
    mask = jnp.concatenate([range_ref[:, cell * CELL : (cell + 1) * CELL] for cell in cells], axis=1)
    sums = dot_nt(jnp.concatenate([mask, mask], axis=1), jnp.concatenate([high, low], axis=1))
    sums_ref[...] = sums[:tiles]
    if first:
        left_ref[...] = sums[tiles : tiles + 1]
        right_ref[...] = sums[tiles + 1 : tiles + 2]
    for copy in copies:
        copy.wait()


def focus(first, cells, places, pulses, width, tiles, tables, sources, more):
    me, forward, inverse, spectra, pulse_mask, range_mask = tables
    pulse_tiles = pulse_mask.shape[0]
    part = pulses // RADIX
    offsets = list(sources)
    vmem = pl.BlockSpec(memory_space=pltpu.VMEM)
    anywhere = pl.BlockSpec(memory_space=pl.ANY)
    in_specs = [pl.BlockSpec(memory_space=pltpu.SMEM)] + [vmem] * (5 + len(offsets))
    shapes = [jax.ShapeDtypeStruct((part, RADIX, 2, width), BF16)]
    shapes += [jax.ShapeDtypeStruct((tiles, pulse_tiles), F32)]
    if first:
        shapes += [jax.ShapeDtypeStruct((1, pulse_tiles), F32)] * 2
    else:
        in_specs += [anywhere]
    direct = all(source.shape[0] % (16 * RADIX) == 0 for source in sources.values())
    x_shape = (RADIX, part, 2 * CELL) if direct else (pulses, 2 * CELL)
    return pl.pallas_call(
        functools.partial(focus_kernel, tuple(offsets), places, tuple(cells), first),
        out_shape=shapes,
        in_specs=in_specs,
        out_specs=[anywhere] + [vmem] * (len(shapes) - 1),
        scratch_shapes=[
            pltpu.VMEM((len(cells),) + x_shape, BF16),
            pltpu.VMEM((len(cells), RADIX, 2, part, CELL), F32),
            pltpu.VMEM((len(cells), RADIX, part, 2 * CELL), BF16),
            pltpu.VMEM((pulses, len(cells) * CELL), BF16),
            pltpu.VMEM((RADIX, part, 2, len(cells) * CELL), BF16),
            pltpu.SemaphoreType.DMA((len(cells), RADIX)),
        ],
        input_output_aliases={} if first else {6 + len(offsets): 0},
        compiler_params=pltpu.CompilerParams(vmem_limit_bytes=FOCUS_VMEM),
        cost_estimate=pl.CostEstimate(
            flops=len(cells) << 31, bytes_accessed=len(cells) << 21, transcendentals=0
        ),
        name="azimuth_focus",
    )(me, forward, inverse, spectra, pulse_mask, range_mask, *sources.values(), *more)


def looks_kernel(from_left_ref, from_right_ref, inside_ref, *refs):
    sums = sum(ref[...] for ref in refs[:-1])
    row = lax.broadcasted_iota(jnp.int32, sums.shape, 0)
    sums += jnp.where(row == 0, from_left_ref[...], 0.0)
    sums += jnp.where(row == sums.shape[0] - 1, from_right_ref[...], 0.0)
    refs[-1][...] = sums / inside_ref[...]


def looks(from_left, from_right, inside, *sums):
    return pl.pallas_call(
        looks_kernel,
        out_shape=jax.ShapeDtypeStruct(inside.shape, F32),
        compiler_params=pltpu.CompilerParams(vmem_limit_bytes=GATE_VMEM),
        cost_estimate=SMALL_COST,
        name="looks",
    )(from_left, from_right, inside, *sums)


def per_device(
    echoes, range_replica, azimuth_replicas, replica_index, azimuth_extent, range_extent
):
    count = lax.axis_size("row")
    device = lax.axis_index("row")
    me = device.astype(jnp.int32)[None]
    rows, _, samples = echoes.shape
    pulses = rows * count
    width = samples // count
    cells = list(range(width // CELL))
    chunked = len(cells) == RADIX and count == 16

    def send(piece, offset):
        if offset == 0:
            return piece
        return lax.ppermute(piece, "row", [(i, i ^ offset) for i in range(count)])

    sibling = send(echoes, 1)
    replica = jnp.pad(range_replica.astype(F32), ((0, 0), (0, min(256, width))))
    if chunked:
        late = ()
        late = (10, 14, 12)
        first = compress_first(me, echoes, replica, [8, 9], width)
        received = {offset: send(piece, offset) for offset, piece in first.items()}
        pieces = compress(me, echoes, sibling, replica, first[8], [12], late, width)
        others = [10, 2, 14, 4, 6, 0]
        pieces.update(compress(me, echoes, sibling, replica, pieces[12][1], others, late, width))
        received.update({offset: send(pieces[offset][0], offset) for offset in [12] + others})
        received_late = {offset: send(pieces[offset][1], offset) for offset in (10, 14, 12)}
    else:
        late = ()
        pieces = compress(me, echoes, sibling, replica, me, list(range(2, count, 2)) + [0], late, width)
        received = {offset: send(piece, offset) for offset, (piece, _) in pieces.items()}

    forward, inverse = (jnp.asarray(m) for m in phase_matrices(pulses))
    tiles = width // TILE
    spectra, pulse_mask, range_mask, inside = make_tables(
        me, azimuth_replicas, replica_index[None, :], azimuth_extent, range_extent, forward, received[0], width
    )
    tables = (me, forward, inverse, spectra, pulse_mask, range_mask)
    early = [cell for cell in cells if not (chunked and cell in LATE)]
    places = {offset: list(range(len(early))) if offset in late else early for offset in received}
    focused, sums, left, right = focus(
        True, early, places, pulses, width, tiles, tables, received, ()
    )
    from_right = lax.ppermute(left, "row", [(i, i - 1) for i in range(1, count)])
    from_left = lax.ppermute(right, "row", [(i, i + 1) for i in range(count - 1)])
    sums = [sums]
    if chunked:
        places = {offset: list(range(len(LATE))) if offset in late else LATE for offset in received}
        sources = {offset: received_late.get(offset, received[offset]) for offset in received}
        focused, late_sums = focus(
            False, LATE, places, pulses, width, tiles, tables, sources, (focused,)
        )
        sums.append(late_sums)
    return focused.reshape(pulses, 2, width), looks(from_left, from_right, inside, *sums)


def solution(mesh):
    return jax.shard_map(
        per_device,
        mesh=mesh,
        in_specs=(
            P(("scene", "row"), None, None),
            P(),
            P(),
            P(("scene", "row")),
            P("scene"),
            P("scene"),
        ),
        out_specs=(P("scene", None, "row"), P(("scene", "row"), None)),
        check_vma=False,
    )
```

```python
import functools

import jax
import jax.numpy as jnp
import ml_dtypes
import numpy as np
from jax import lax
from jax.experimental import pallas as pl
from jax.experimental.pallas import tpu as pltpu
from jax.sharding import PartitionSpec as P

TILE = 16
RADIX = 4
CELL = 128
F32 = jnp.float32
BF16 = jnp.bfloat16
FIRST_VMEM = 24 << 20
RANGE_VMEM = 24 << 20
GATE_VMEM = 1 << 20
FOCUS_VMEM = 24 << 20
SMALL_COST = pl.CostEstimate(flops=1 << 20, bytes_accessed=1 << 16, transcendentals=0)


def dot(a, b):
    return jnp.dot(a, b, preferred_element_type=F32)


def dot_nt(a, b):
    return lax.dot_general(a, b, (((1,), (1,)), ((), ())), preferred_element_type=F32)


def split(x):
    high = x.astype(BF16)
    low = (x - high.astype(F32)).astype(BF16)
    return high, low


def twice(x):
    return jnp.concatenate([x, x], axis=0)


def two_terms(matrix):
    high = matrix.astype(ml_dtypes.bfloat16)
    low = (matrix - high.astype(np.float64)).astype(ml_dtypes.bfloat16)
    return np.concatenate([high, low], axis=2)


@functools.lru_cache(maxsize=None)
def phase_matrices(length):
    part = length // RADIX
    index = np.arange(part)
    k = index.reshape(part // RADIX, RADIX).T.reshape(-1)
    step = np.arange(RADIX)[:, None, None]
    phase = (k[None, :, None] * (RADIX * index[None, None, :] + step)) % length
    angle = phase * (2.0 * np.pi / length)
    cos, sin = np.cos(angle), np.sin(angle)
    forward = two_terms(np.concatenate([cos, -sin], axis=1))
    inverse = two_terms(np.concatenate([cos, sin], axis=2).reshape(RADIX, part, 2, part).transpose(0, 2, 3, 1).reshape(RADIX, 2 * part, part))
    return forward, inverse


def complex_product(matrix, x):
    product = dot(matrix, twice(x))
    rows, lanes = product.shape[0] // 2, product.shape[1] // 2
    real = product[:rows, :lanes] - product[rows:, lanes:]
    imag = product[:rows, lanes:] + product[rows:, :lanes]
    return real, imag


def butterfly(x, sign):
    (ar, ai), (br, bi), (cr, ci), (dr, di) = x
    pr, pi, mr, mi = ar + cr, ai + ci, ar - cr, ai - ci
    sr, si, tr, ti = br + dr, bi + di, br - dr, bi - di
    if sign < 0:
        tr, ti = ti, -tr
    else:
        tr, ti = -ti, tr
    return [(pr + sr, pi + si), (mr + tr, mi + ti), (pr - sr, pi - si), (mr - tr, mi - ti)]


def spectrum_part(values, r):
    rows = values[0][0].shape[0] // RADIX
    span = slice(r * rows, (r + 1) * rows)
    parts = butterfly([(re[span], im[span]) for re, im in values], -1)
    return [jnp.concatenate([p[c] for p in parts], axis=0) for c in range(2)]


def table_kernel(h_ref, table):
    block = table.shape[1]
    for part in range(2):
        lines = jnp.broadcast_to(h_ref[part : part + 1], (block, h_ref.shape[1]))
        table[part] = pltpu.roll(lines, 0, 1, stride=1, stride_axis=0).astype(BF16)


def windows(x_refs, base, width, blocks, count):
    pieces = []
    for step in range(blocks):
        place = base + step
        start = pl.multiple_of(jnp.minimum(place, count - 1) * width, width)
        pieces.append([x_ref.at[:, :, pl.ds(start, width)] for x_ref in x_refs])
    return pieces


def pulse_order(total, swapped):
    row = lax.broadcasted_iota(jnp.int32, (2 * total, 2 * total), 0)
    column = lax.broadcasted_iota(jnp.int32, (2 * total, 2 * total), 1)
    quarter = total // RADIX
    pulse = RADIX * (row % quarter) + (row % total) // quarter
    source = 2 * pulse + row // total
    source = jnp.where(swapped, (source + total) % (2 * total), source)
    return (column == source).astype(F32).astype(BF16)


def correlate(window, table, width, early_out, late_out):
    block = table.shape[1]
    taps = table.shape[2] - block
    total = window.shape[0] // 2
    stacked = jnp.concatenate(
        [window[:, j * block : j * block + block + taps] for j in range(width // block)], axis=0
    )
    with_real = dot_nt(stacked, table[0])
    with_imag = dot_nt(stacked, table[1])
    placed = [0, 0]
    for cell in range(width // CELL):
        at = 2 * total * (cell * CELL // block)
        re, im = slice(at, at + total), slice(at + total, at + 2 * total)
        lanes = slice(cell * CELL % block, cell * CELL % block + CELL)
        real = with_real[re, lanes] + with_imag[im, lanes]
        imag = with_real[im, lanes] - with_imag[re, lanes]
        late = late_out is not None and cell in LATE
        out = late_out if late else early_out
        place = placed[late]
        placed[late] += 1
        out[:, 2 * CELL * place : 2 * CELL * (place + 1)] = jnp.concatenate(
            [real.astype(BF16), imag.astype(BF16)], axis=1
        )


def first_range_kernel(offsets, width, me_ref, x_hbm, h_ref, *refs):
    outs, (table, x_ref, sems) = refs[:-3], refs[-3:]
    rows = x_hbm.shape[0]
    count = x_hbm.shape[2] // width
    blocks = x_ref.shape[0]
    me = me_ref[0]
    base = me ^ offsets[0]
    base = base - base % 2
    copies = []
    for step, (piece,) in enumerate(windows([x_hbm], base, width, blocks, count)):
        copies.append(pltpu.make_async_copy(piece, x_ref.at[step], sems.at[step]))
    for copy in copies:
        copy.start()
    table_kernel(h_ref, table)
    order = pulse_order(rows, False)
    for copy in copies:
        copy.wait()
    pieces = []
    for step in range(blocks):
        piece = x_ref[step].reshape(2 * rows, width)
        pieces.append(jnp.where(base + step < count, piece, jnp.zeros_like(piece)))
    window = dot(order, jnp.concatenate(pieces, axis=1)).astype(BF16)
    reach = window.shape[1] - width
    for offset, out in zip(offsets, outs):
        odd = (me ^ offset) % 2
        mine = jnp.where(odd == 0, window[:, :reach], window[:, width:])
        correlate(mine, table, width, out, None)


def range_kernel(offsets, late, width, me_ref, x_ref, sibling_ref, h_ref, after_ref, *refs):
    del after_ref
    outs, table = refs[:-1], refs[-1]
    table_kernel(h_ref, table)
    rows = x_ref.shape[0]
    taps = table.shape[2] - table.shape[1]
    count = x_ref.shape[2] // width
    me = me_ref[0]
    order = pulse_order(2 * rows, me % 2 == 1)
    outs = iter(outs)
    for offset in offsets:
        owner = me ^ offset
        pieces = []
        for step, piece in enumerate(
            windows([x_ref, sibling_ref], owner, width, 1 + -(-taps // width), count)
        ):
            piece = jnp.concatenate([part[...].reshape(2 * rows, width) for part in piece], axis=0)
            if step:
                piece = jnp.where(owner + step < count, piece, jnp.zeros_like(piece))
            pieces.append(piece)
        window = dot(order, jnp.concatenate(pieces, axis=1)).astype(BF16)
        early_out = next(outs)
        late_out = next(outs) if offset in late else None
        correlate(window, table, width, early_out, late_out)


LATE = (1, 2)


def compress_first(me, echoes, replica, offsets, width):
    rows = echoes.shape[0]
    block = min(256, width)
    taps = replica.shape[1] - block
    blocks = 2 + -(-taps // width)
    vmem = pl.BlockSpec(memory_space=pltpu.VMEM)
    outs = pl.pallas_call(
        functools.partial(first_range_kernel, tuple(offsets), width),
        out_shape=[jax.ShapeDtypeStruct((rows, 2 * width), BF16)] * len(offsets),
        in_specs=[pl.BlockSpec(memory_space=pltpu.SMEM), pl.BlockSpec(memory_space=pl.ANY), vmem],
        out_specs=[vmem] * len(offsets),
        scratch_shapes=[
            pltpu.VMEM((2, block, taps + block), BF16),
            pltpu.VMEM((blocks, rows, 2, width), BF16),
            pltpu.SemaphoreType.DMA((blocks,)),
        ],
        compiler_params=pltpu.CompilerParams(vmem_limit_bytes=FIRST_VMEM),
        cost_estimate=pl.CostEstimate(
            flops=len(offsets) * 16 * rows * width * (taps + 256),
            bytes_accessed=len(offsets) * 4 * rows * width * 3,
            transcendentals=0,
        ),
        name="range_compress_first",
    )(me, echoes, replica)
    return dict(zip(offsets, outs))


def compress(me, echoes, sibling, replica, after, offsets, late, width):
    total = 2 * echoes.shape[0]
    block = min(256, width)
    taps = replica.shape[1] - block
    vmem = pl.BlockSpec(memory_space=pltpu.VMEM)
    shapes = []
    for offset in offsets:
        if offset in late:
            shapes += [(total, 2 * (width - len(LATE) * CELL)), (total, 2 * len(LATE) * CELL)]
        else:
            shapes += [(total, 2 * width)]
    outs = pl.pallas_call(
        functools.partial(range_kernel, tuple(offsets), late, width),
        out_shape=[jax.ShapeDtypeStruct(shape, BF16) for shape in shapes],
        in_specs=[pl.BlockSpec(memory_space=pltpu.SMEM), vmem, vmem, vmem, pl.BlockSpec(memory_space=pl.ANY)],
        out_specs=[vmem] * len(shapes),
        scratch_shapes=[pltpu.VMEM((2, block, taps + block), BF16)],
        compiler_params=pltpu.CompilerParams(vmem_limit_bytes=RANGE_VMEM),
        cost_estimate=pl.CostEstimate(
            flops=len(offsets) * 16 * total * width * (taps + block),
            bytes_accessed=len(offsets) * 4 * total * width * 3,
            transcendentals=0,
        ),
        name="range_compress",
    )(me, echoes, sibling, replica, after)
    outs = iter(outs)
    return {offset: (next(outs), next(outs) if offset in late else None) for offset in offsets}


def gate_kernel(*refs):
    del refs


def gate(pieces, after):
    anywhere = pl.BlockSpec(memory_space=pl.ANY)
    return pl.pallas_call(
        gate_kernel,
        out_shape=[jax.ShapeDtypeStruct(piece.shape, piece.dtype) for piece in pieces],
        in_specs=[anywhere] * (len(pieces) + len(after)),
        out_specs=[anywhere] * len(pieces),
        input_output_aliases={n: n for n in range(len(pieces))},
        compiler_params=pltpu.CompilerParams(vmem_limit_bytes=GATE_VMEM),
        cost_estimate=SMALL_COST,
        name="gate",
    )(*pieces, *after)


def column(line, select):
    return jnp.sum(jnp.where(select, line, 0.0), axis=1, keepdims=True)


def tables_kernel(
    me_ref, taps_ref, index_ref, azimuth_ref, range_ref, matrix_ref, after_ref,
    spectra_ref, pulse_ref, mask_ref, inside_ref,
):
    del after_ref
    part = matrix_ref.shape[1] // 2
    length = part * RADIX
    replicas, _, tap_count = taps_ref.shape
    row = lax.broadcasted_iota(jnp.int32, (2 * CELL, 2 * replicas), 0)
    source = lax.broadcasted_iota(jnp.int32, (2 * CELL, 2 * replicas), 1)
    place = (row % CELL < replicas) & (source == 2 * (row % CELL) + row // CELL)
    taps = taps_ref[...].reshape(2 * replicas, tap_count)
    taps = dot(place.astype(F32).astype(BF16), taps).astype(BF16)
    m = lax.broadcasted_iota(jnp.int32, (part, tap_count), 0)
    tap = lax.broadcasted_iota(jnp.int32, (part, tap_count), 1)
    bins = index_ref.shape[1]
    row = lax.broadcasted_iota(jnp.int32, (2 * replicas, bins), 0)
    chosen = (row % replicas == index_ref[...]).astype(F32).astype(BF16)
    values = []
    for q in range(RADIX):
        pick = (tap == RADIX * m + q).astype(F32).astype(BF16)
        values.append(complex_product(matrix_ref[q], dot_nt(pick, taps).astype(BF16)))
    for r in range(RADIX):
        spectrum = jnp.concatenate(spectrum_part(values, r), axis=0) * (1.0 / length)
        high, low = split(spectrum)
        both = jnp.concatenate([high[:, :replicas], low[:, :replicas]], axis=1)
        spectra_ref[r] = dot(both, chosen)

    def mask(starts, stops, at):
        at = at.astype(F32)
        return ((at >= starts) & (at < stops)).astype(F32).astype(BF16)

    pulse_tiles = azimuth_ref.shape[1]
    extents = azimuth_ref[...].astype(F32)
    row = lax.broadcasted_iota(jnp.int32, (pulse_tiles, pulse_tiles), 0)
    lane = lax.broadcasted_iota(jnp.int32, (pulse_tiles, pulse_tiles), 1)
    extent = column(extents, row == lane)
    start = (TILE * lax.broadcasted_iota(jnp.int32, (pulse_tiles, 1), 0)).astype(F32)
    lane = lax.broadcasted_iota(jnp.int32, pulse_ref.shape, 1)
    pulse_ref[...] = mask(start - extent, start + TILE + extent, RADIX * (lane % part) + lane // part)
    start = (TILE * lax.broadcasted_iota(jnp.int32, (1, pulse_tiles), 1)).astype(F32)
    pulse_count = jnp.minimum(start + TILE + extents, 1.0 * length) - jnp.maximum(start - extents, 0.0)

    tiles = inside_ref.shape[0]
    mask_rows, width = mask_ref.shape
    total = range_ref.shape[1]
    row = lax.broadcasted_iota(jnp.int32, (mask_rows, 1), 0)
    tile = me_ref[0] * tiles + jnp.where(row == tiles, -1, jnp.where(row == tiles + 1, tiles, row))
    exists = (row < tiles + 2) & (tile >= 0) & (tile < total)
    lane = lax.broadcasted_iota(jnp.int32, (mask_rows, total), 1)
    extent = column(range_ref[...].astype(F32), lane == tile)
    start = (TILE * tile).astype(F32) - extent
    stop = (TILE * tile + TILE).astype(F32) + extent
    lane = lax.broadcasted_iota(jnp.int32, mask_ref.shape, 1)
    mask_ref[...] = mask(start, jnp.where(exists, stop, start), me_ref[0] * width + lane)
    count = jnp.minimum(stop, 1.0 * TILE * total) - jnp.maximum(start, 0.0)
    inside_ref[...] = count[:tiles] * pulse_count


def make_tables(me, azimuth_replicas, index, azimuth_extent, range_extent, matrix, after, width):
    part = matrix.shape[1] // 2
    replicas = azimuth_replicas.shape[0]
    pulse_tiles = azimuth_extent.shape[0]
    tiles = width // TILE
    mask_rows = -(-(tiles + 2) // 16) * 16
    vmem = pl.BlockSpec(memory_space=pltpu.VMEM)
    shapes = [
        ((RADIX, 2 * part, width), F32),
        ((pulse_tiles, RADIX * part), BF16),
        ((mask_rows, width), BF16),
        ((tiles, pulse_tiles), F32),
    ]
    return pl.pallas_call(
        tables_kernel,
        out_shape=[jax.ShapeDtypeStruct(*shape) for shape in shapes],
        in_specs=[pl.BlockSpec(memory_space=pltpu.SMEM)] + [vmem] * 5 + [pl.BlockSpec(memory_space=pl.ANY)],
        out_specs=[vmem] * 4,
        compiler_params=pltpu.CompilerParams(vmem_limit_bytes=RANGE_VMEM),
        cost_estimate=pl.CostEstimate(flops=1 << 31, bytes_accessed=4 << 20, transcendentals=0),
        name="tables",
    )(me, azimuth_replicas, index, azimuth_extent[None, :], range_extent[None, :], matrix, after)


def gather_pulses(offsets, places, n, sources, me, total, x_ref):
    direct = x_ref.shape[0] == RADIX
    for offset, source in zip(offsets, sources):
        at = slice(2 * CELL * places[offset][n], 2 * CELL * (places[offset][n] + 1))
        rows = source.shape[0]
        owner = (me ^ offset) // (2 * rows // total)
        rows = rows // RADIX if direct else rows
        start = pl.multiple_of(owner * rows, rows)
        if direct:
            for q in range(RADIX):
                span = slice(q * rows, (q + 1) * rows)
                x_ref[q, pl.ds(start, rows), :] = source[span, at]
        else:
            x_ref[pl.ds(start, rows), :] = source[:, at]


def pulses_of(x_ref, q, total, part):
    if x_ref.shape[0] == RADIX:
        return x_ref[q]
    quarter = total // RADIX
    m = lax.broadcasted_iota(jnp.int32, (part, x_ref.shape[0]), 0)
    row = lax.broadcasted_iota(jnp.int32, (part, x_ref.shape[0]), 1)
    pick = row == (m // quarter) * total + q * quarter + m % quarter
    return dot(pick.astype(F32).astype(BF16), x_ref[...]).astype(BF16)


def focus_kernel(
    offsets, places, cells, first, me_ref, forward_ref, inverse_ref, spectra_ref, pulse_ref, range_ref, *refs
):
    sources, refs = refs[: len(offsets)], refs[len(offsets) :]
    if first:
        focused_hbm, sums_ref, left_ref, right_ref = refs[:4]
        tiles = sums_ref.shape[0]
    else:
        _, focused_hbm, sums_ref = refs[:3]
        tiles = sums_ref.shape[0]
    x_ref, v_ref, s_ref, power_ref, image_ref, sems = refs[-6:]
    total = max(source.shape[0] for source in sources)
    part = v_ref.shape[3]
    me = me_ref[0]
    steps = range(len(cells))

    def transform(n):
        for q in range(RADIX):
            x = pulses_of(x_ref.at[n], q, total, part)
            v_ref[n, q, 0], v_ref[n, q, 1] = complex_product(forward_ref[q], x)

    def correlate_cell(n):
        lanes = slice(cells[n] * CELL, (cells[n] + 1) * CELL)
        rows = part // RADIX
        for r in range(RADIX):
            span = slice(r * rows, (r + 1) * rows)
            x = butterfly([(v_ref[n, q, 0, span], v_ref[n, q, 1, span]) for q in range(RADIX)], -1)
            y = []
            for j, (sr, si) in enumerate(x):
                gr = spectra_ref[r, j * rows : (j + 1) * rows, lanes]
                gi = spectra_ref[r, part + j * rows : part + (j + 1) * rows, lanes]
                y.append((sr * gr + si * gi, si * gr - sr * gi))
            for q, (re, im) in enumerate(butterfly(y, 1)):
                s_ref[n, q, span, :CELL] = re.astype(BF16)
                s_ref[n, q, span, CELL:] = im.astype(BF16)

    copies = []

    def finish(n):
        lanes = slice(n * CELL, (n + 1) * CELL)
        for q in range(RADIX):
            re, im = complex_product(inverse_ref[q], s_ref[n, q])
            both = jnp.stack([re.astype(BF16), im.astype(BF16)], axis=0)
            image_ref[q, :, :, lanes] = jnp.swapaxes(both, 0, 1)
            power_ref[q * part : (q + 1) * part, lanes] = (re * re + im * im).astype(BF16)
            copy = pltpu.make_async_copy(
                image_ref.at[q, :, :, lanes],
                focused_hbm.at[:, q, :, cells[n] * CELL : (cells[n] + 1) * CELL],
                sems.at[n, q],
            )
            copy.start()
            copies.append(copy)

    for n in steps:
        gather_pulses(offsets, places, n, sources, me, total, x_ref.at[n])
        transform(n)
    for n in steps:
        correlate_cell(n)
        finish(n)
    sums = dot(pulse_ref[...], power_ref[...])
    high, low = split(sums)
    mask = jnp.concatenate([range_ref[:, cell * CELL : (cell + 1) * CELL] for cell in cells], axis=1)
    sums = dot_nt(jnp.concatenate([mask, mask], axis=1), jnp.concatenate([high, low], axis=1))
    sums_ref[...] = sums[:tiles]
    if first:
        left_ref[...] = sums[tiles : tiles + 1]
        right_ref[...] = sums[tiles + 1 : tiles + 2]
    for copy in copies:
        copy.wait()


def focus(first, cells, places, pulses, width, tiles, tables, sources, more):
    me, forward, inverse, spectra, pulse_mask, range_mask = tables
    pulse_tiles = pulse_mask.shape[0]
    part = pulses // RADIX
    offsets = list(sources)
    vmem = pl.BlockSpec(memory_space=pltpu.VMEM)
    anywhere = pl.BlockSpec(memory_space=pl.ANY)
    in_specs = [pl.BlockSpec(memory_space=pltpu.SMEM)] + [vmem] * (5 + len(offsets))
    shapes = [jax.ShapeDtypeStruct((part, RADIX, 2, width), BF16)]
    shapes += [jax.ShapeDtypeStruct((tiles, pulse_tiles), F32)]
    if first:
        shapes += [jax.ShapeDtypeStruct((1, pulse_tiles), F32)] * 2
    else:
        in_specs += [anywhere]
    direct = all(source.shape[0] % (16 * RADIX) == 0 for source in sources.values())
    x_shape = (RADIX, part, 2 * CELL) if direct else (pulses, 2 * CELL)
    return pl.pallas_call(
        functools.partial(focus_kernel, tuple(offsets), places, tuple(cells), first),
        out_shape=shapes,
        in_specs=in_specs,
        out_specs=[anywhere] + [vmem] * (len(shapes) - 1),
        scratch_shapes=[
            pltpu.VMEM((len(cells),) + x_shape, BF16),
            pltpu.VMEM((len(cells), RADIX, 2, part, CELL), F32),
            pltpu.VMEM((len(cells), RADIX, part, 2 * CELL), BF16),
            pltpu.VMEM((pulses, len(cells) * CELL), BF16),
            pltpu.VMEM((RADIX, part, 2, len(cells) * CELL), BF16),
            pltpu.SemaphoreType.DMA((len(cells), RADIX)),
        ],
        input_output_aliases={} if first else {6 + len(offsets): 0},
        compiler_params=pltpu.CompilerParams(vmem_limit_bytes=FOCUS_VMEM),
        cost_estimate=pl.CostEstimate(
            flops=len(cells) << 31, bytes_accessed=len(cells) << 21, transcendentals=0
        ),
        name="azimuth_focus",
    )(me, forward, inverse, spectra, pulse_mask, range_mask, *sources.values(), *more)


def looks_kernel(from_left_ref, from_right_ref, inside_ref, *refs):
    sums = sum(ref[...] for ref in refs[:-1])
    row = lax.broadcasted_iota(jnp.int32, sums.shape, 0)
    sums += jnp.where(row == 0, from_left_ref[...], 0.0)
    sums += jnp.where(row == sums.shape[0] - 1, from_right_ref[...], 0.0)
    refs[-1][...] = sums / inside_ref[...]


def looks(from_left, from_right, inside, *sums):
    return pl.pallas_call(
        looks_kernel,
        out_shape=jax.ShapeDtypeStruct(inside.shape, F32),
        compiler_params=pltpu.CompilerParams(vmem_limit_bytes=GATE_VMEM),
        cost_estimate=SMALL_COST,
        name="looks",
    )(from_left, from_right, inside, *sums)


def per_device(
    echoes, range_replica, azimuth_replicas, replica_index, azimuth_extent, range_extent
):
    count = lax.axis_size("row")
    device = lax.axis_index("row")
    me = device.astype(jnp.int32)[None]
    rows, _, samples = echoes.shape
    pulses = rows * count
    width = samples // count
    cells = list(range(width // CELL))
    chunked = len(cells) == RADIX and count == 16

    def send(piece, offset):
        if offset == 0:
            return piece
        return lax.ppermute(piece, "row", [(i, i ^ offset) for i in range(count)])

    sibling = send(echoes, 1)
    replica = jnp.pad(range_replica.astype(F32), ((0, 0), (0, min(256, width))))
    if chunked:
        late = ()
        late = (10, 14, 12)
        first = compress_first(me, echoes, replica, [8, 9], width)
        received = {offset: send(piece, offset) for offset, piece in first.items()}
        pieces = compress(me, echoes, sibling, replica, first[8], [12], late, width)
        others = [10, 2, 14, 4, 6, 0]
        pieces.update(compress(me, echoes, sibling, replica, pieces[12][1], others, late, width))
        received.update({offset: send(pieces[offset][0], offset) for offset in [12] + others})
        received_late = {offset: send(pieces[offset][1], offset) for offset in (10, 14, 12)}
    else:
        late = ()
        pieces = compress(me, echoes, sibling, replica, me, list(range(2, count, 2)) + [0], late, width)
        received = {offset: send(piece, offset) for offset, (piece, _) in pieces.items()}

    forward, inverse = (jnp.asarray(m) for m in phase_matrices(pulses))
    tiles = width // TILE
    spectra, pulse_mask, range_mask, inside = make_tables(
        me, azimuth_replicas, replica_index[None, :], azimuth_extent, range_extent, forward, received[0], width
    )
    tables = (me, forward, inverse, spectra, pulse_mask, range_mask)
    early = [cell for cell in cells if not (chunked and cell in LATE)]
    places = {offset: list(range(len(early))) if offset in late else early for offset in received}
    focused, sums, left, right = focus(
        True, early, places, pulses, width, tiles, tables, received, ()
    )
    from_right = lax.ppermute(left, "row", [(i, i - 1) for i in range(1, count)])
    from_left = lax.ppermute(right, "row", [(i, i + 1) for i in range(count - 1)])
    sums = [sums]
    if chunked:
        places = {offset: list(range(len(LATE))) if offset in late else LATE for offset in received}
        sources = {offset: received_late.get(offset, received[offset]) for offset in received}
        focused, late_sums = focus(
            False, LATE, places, pulses, width, tiles, tables, sources, (focused,)
        )
        sums.append(late_sums)
    return focused.reshape(pulses, 2, width), looks(from_left, from_right, inside, *sums)


def solution(mesh):
    return jax.shard_map(
        per_device,
        mesh=mesh,
        in_specs=(
            P(("scene", "row"), None, None),
            P(),
            P(),
            P(("scene", "row")),
            P("scene"),
            P("scene"),
        ),
        out_specs=(P("scene", None, "row"), P(("scene", "row"), None)),
        check_vma=False,
    )
```
